32 devices in a mesh: batch: 16 (over z, x, core), seq: 2 (over y).
Axes of the slice: x: 2, y: 2, z: 4, core: 2. Of those that a mesh axis runs over, the one named last changes fastest.
Arguments:
- tokens: bfloat16 [16, 512, 768], P('batch', 'seq'), may hold values from -6 to 6
- segment_ids: int32 [16, 512], P('batch'), may hold values from 0 to 32, as said below
- w_query: bfloat16 [768, 768], replicated, may hold values from -0.21875 to 0.21875
- b_query: float32 [768], replicated, may hold values from -3 to 3
- w_key: bfloat16 [768, 768], replicated, may hold values from -0.21875 to 0.21875
- w_value: bfloat16 [768, 768], replicated, may hold values from -0.21875 to 0.21875
- b_value: float32 [768], replicated, may hold values from -3 to 3
- w_out: bfloat16 [768, 768], replicated, may hold values from -2 to 2
- b_out: float32 [768], replicated, may hold values from -3 to 3
- gain_attn: float32 [768], replicated, may hold values from 0.5 to 1.5
- shift_attn: float32 [768], replicated, may hold values from -2 to 2
- w_up: bfloat16 [768, 3072], replicated, may hold values from -0.21875 to 0.21875
- b_up: float32 [3072], replicated, may hold values from -3 to 3
- w_down: bfloat16 [3072, 768], replicated, may hold values from -0.109375 to 0.109375
- b_down: float32 [768], replicated, may hold values from -3 to 3
- gain_ffn: float32 [768], replicated, may hold values from 0.5 to 1.5
- shift_ffn: float32 [768], replicated, may hold values from -2 to 2
- w_head: bfloat16 [768], replicated, may hold values from -0.21875 to 0.21875
- cot_out: bfloat16 [16, 512, 768], P('batch', 'seq'), may hold values from -6 to 6
- cot_weight: float32 [16, 512], P('batch', 'seq'), may hold values from -6 to 6
Outputs:
- layer_out: bfloat16 [16, 512, 768], P('batch', 'seq')
- term_weight: float32 [16, 512], P('batch', 'seq')
- grad_tokens: float32 [16, 512, 768], P('batch', 'seq')
- grad_w_query: float32 [768, 768], replicated
- grad_b_query: float32 [768], replicated
- grad_w_key: float32 [768, 768], replicated
- grad_w_value: float32 [768, 768], replicated
- grad_b_value: float32 [768], replicated
- grad_w_out: float32 [768, 768], replicated
- grad_b_out: float32 [768], replicated
- grad_gain_attn: float32 [768], replicated
- grad_shift_attn: float32 [768], replicated
- grad_w_up: float32 [768, 3072], replicated
- grad_b_up: float32 [3072], replicated
- grad_w_down: float32 [3072, 768], replicated
- grad_b_down: float32 [768], replicated
- grad_gain_ffn: float32 [768], replicated
- grad_shift_ffn: float32 [768], replicated
- grad_w_head: float32 [768], replicated
The draws below stay inside these ranges and needn't reach their ends.
Inputs may be any that keep to these rules, and one draw needn't show every extreme that they name: `segment_ids`: in each row the ids start at 0, never fall, and rise by at most one from a position to the next; no new id begins within 64 positions of the row's middle; some row reaches the largest id.
All inputs are finite; a program needn't handle non-finite values.
Results may differ from the reference program's by a relative error of at most 0.023.
Values may be sent and summed in bfloat16 or wider, within the bound.
No kernel may reach another device: no remote copies, remote signals or barrier semaphores. Data moves between devices by JAX's collectives and lax.ppermute only.
A program may use at most 384 MiB of HBM per device.

```python
import math
import jax
import jax.numpy as jnp
from jax import lax

D = 768
HD = 64
FF = 3072
LEN = 512
ROWS = 16


def draw_segment_ids(key, part):
    key = jax.random.fold_in(key, 7)
    start_key, row_key = jax.random.split(key)
    starts = jax.random.randint(start_key, (ROWS, LEN), 0, 80) == 0
    position = jnp.arange(LEN)
    middle = (position >= LEN // 2 - LEN // 8) & (position < LEN // 2 + LEN // 8)
    chosen_row = jax.random.randint(row_key, (), 0, ROWS)
    forced = (jnp.arange(ROWS)[:, None] == chosen_row) & (position % 4 == 0)[None, :]
    opened = (starts | forced) & jnp.logical_not(middle) & (position > 0)
    counted = jnp.cumsum(opened.astype(jnp.int32), axis=1)
    return jnp.minimum(counted, LEN // 16).astype(jnp.int32)


def levels(key, extent, pieces, least, high):
    def one(dim, blocks):
        draws = jax.random.uniform(jax.random.fold_in(jax.random.fold_in(key, 6), dim), (blocks,), jnp.float32, least / len(pieces), high / len(pieces))
        return jnp.repeat(jnp.exp(draws), extent[dim] // blocks).reshape((-1,) + (1,) * (len(extent) - dim - 1))

    level = one(*pieces[0])
    for cut in pieces[1:]:
        level = level * one(*cut)
    return level


def gaussian(stream_key, extent, spread, most, cuts=(), dtype=jnp.bfloat16):
    factor_of = levels(stream_key, extent, cuts, -0.22, 0.18) if cuts else 1.0
    array = jax.random.normal(stream_key, extent, jnp.float32) * spread * factor_of
    return jnp.minimum(jnp.maximum(array, -most), most).astype(dtype)


def setup_inputs(seed: int = 0) -> dict:
    arg_keys = jax.random.split(jax.random.key(seed), 21)
    tokens = gaussian(arg_keys[0], (ROWS, LEN, D), 1.0, 6.0, ((0, 16), (1, 2)))
    segment_ids = draw_segment_ids(jax.random.fold_in(arg_keys[20], 71), 0)
    w_query = gaussian(arg_keys[2], (D, D), D ** -0.5, 0.21875)
    b_query = gaussian(arg_keys[3], (D,), 0.5, 3.0, (), jnp.float32)
    w_key = gaussian(arg_keys[4], (D, D), D ** -0.5, 0.21875)
    w_value = gaussian(arg_keys[5], (D, D), D ** -0.5, 0.21875)
    b_value = gaussian(arg_keys[6], (D,), 0.5, 3.0, (), jnp.float32)
    w_out = gaussian(arg_keys[7], (D, D), (max(1, D // 80)) ** -0.5, 2.0)
    b_out = gaussian(arg_keys[8], (D,), 0.5, 3.0, (), jnp.float32)
    gain_attn = jnp.clip(1.0 + 0.1 * jax.random.normal(arg_keys[9], (D,), jnp.float32), 0.5, 1.5)
    shift_attn = gaussian(arg_keys[10], (D,), 0.3, 2.0, (), jnp.float32)
    w_up = gaussian(arg_keys[11], (D, FF), D ** -0.5, 0.21875)
    b_up = gaussian(arg_keys[12], (FF,), 0.5, 3.0, (), jnp.float32)
    w_down = gaussian(arg_keys[13], (FF, D), FF ** -0.5, 0.109375)
    b_down = gaussian(arg_keys[14], (D,), 0.5, 3.0, (), jnp.float32)
    gain_ffn = jnp.clip(1.0 + 0.1 * jax.random.normal(arg_keys[15], (D,), jnp.float32), 0.5, 1.5)
    shift_ffn = gaussian(arg_keys[16], (D,), 0.3, 2.0, (), jnp.float32)
    w_head = gaussian(arg_keys[17], (D,), D ** -0.5, 0.21875)
    cot_out = gaussian(arg_keys[18], (ROWS, LEN, D), 1.0, 6.0, ((0, 16), (1, 2)))
    cot_weight = gaussian(arg_keys[19], (ROWS, LEN), 1.0, 6.0, ((0, 16), (1, 2)), jnp.float32)
    return {"tokens": tokens, "segment_ids": segment_ids, "w_query": w_query, "b_query": b_query, "w_key": w_key, "w_value": w_value, "b_value": b_value, "w_out": w_out, "b_out": b_out, "gain_attn": gain_attn, "shift_attn": shift_attn, "w_up": w_up, "b_up": b_up, "w_down": w_down, "b_down": b_down, "gain_ffn": gain_ffn, "shift_ffn": shift_ffn, "w_head": w_head, "cot_out": cot_out, "cot_weight": cot_weight}


@jax.custom_vjp
def low(v):
    return lax.optimization_barrier(v.astype(jnp.bfloat16)).astype(jnp.float32)

@jax.custom_vjp
def low_back(v):
    return v

def low_keep(v):
    return (low(v), None)

def low_pass(kept, grad):
    return (grad,)

def back_keep(v):
    return (v, None)

def back_low(kept, grad):
    return (low(grad),)
low.defvjp(low_keep, low_pass)
low_back.defvjp(back_keep, back_low)
masked = -1e+30
eps_norm = 1e-06
highest = lax.Precision.HIGHEST

def both_round(values):
    return low_back(low(values))

def matmul(left, right):
    return jnp.dot(left, right, precision=highest, preferred_element_type=jnp.float32)

def layer_norm(values, gain, shift):
    centered = values - lax.optimization_barrier(jnp.mean(values, -1, keepdims=True))
    inverse = lax.rsqrt(lax.optimization_barrier(jnp.mean(centered * centered, -1, keepdims=True)) + eps_norm)
    return centered * inverse * gain + shift

def layer_rows(inputs, segments, params):
    w_query, b_query, w_key, w_value, b_value, w_out, b_out, gain_attn, shift_attn, w_up, b_up, w_down, b_down, gain_ffn, shift_ffn, w_head = params
    row_count, seq_len, model_width = inputs.shape
    token_rows = inputs.reshape(-1, model_width)
    head_shape = (row_count, seq_len, model_width // HD, HD)
    query_heads = both_round(matmul(token_rows, w_query) + b_query).reshape(head_shape)
    key_heads = both_round(matmul(token_rows, w_key)).reshape(head_shape)
    value_heads = both_round(matmul(token_rows, w_value) + b_value).reshape(head_shape)
    scores = jnp.einsum('rqhd,rkhd->rhqk', query_heads, key_heads, precision=highest) * HD ** (-0.5)
    allowed = (segments[:, :, None] == segments[:, None, :])[:, None]
    scores = low_back(jnp.where(allowed, scores, masked))
    attn_probs = jax.nn.softmax(scores, axis=-1)
    attended = jnp.einsum('rhqk,rkhd->rqhd', low(attn_probs), value_heads, precision=highest)
    attended = attended.reshape(-1, model_width)
    attn_out = low_back(matmul(both_round(attended), w_out) + b_out)
    first_norm = layer_norm(token_rows + attn_out, gain_attn, shift_attn)
    upper_pre = low_back(matmul(low(first_norm), w_up) + b_up)
    activated = low(jax.nn.gelu(upper_pre, approximate=False))
    down_out = low_back(matmul(activated, w_down) + b_down)
    second_norm = layer_norm(first_norm + down_out, gain_ffn, shift_ffn)
    term_weight = jax.nn.softplus(jnp.dot(second_norm, w_head, precision=highest))
    return (second_norm.reshape(row_count, seq_len, model_width), term_weight.reshape(row_count, seq_len))

def reference(tokens, segment_ids, w_query, b_query, w_key, w_value, b_value, w_out, b_out, gain_attn, shift_attn, w_up, b_up, w_down, b_down, gain_ffn, shift_ffn, w_head, cot_out, cot_weight):
    params = tuple((item.astype(jnp.float32) for item in (w_query, b_query, w_key, w_value, b_value, w_out, b_out, gain_attn, shift_attn, w_up, b_up, w_down, b_down, gain_ffn, shift_ffn, w_head)))
    row_group = math.gcd(ROWS, 8)
    group_count = ROWS // row_group
    checked = jax.checkpoint(layer_rows)

    def forward(inputs, weights_all):

        def one_block(operands):
            return checked(operands[0], operands[1], weights_all)
        outputs, terms = lax.map(one_block, (inputs.reshape(group_count, row_group, LEN, D), segment_ids.reshape(group_count, row_group, LEN)))
        return (outputs.reshape(ROWS, LEN, D), terms.reshape(ROWS, LEN))
    (layer_out, term_weight), pullback = jax.vjp(forward, tokens.astype(jnp.float32), params)
    grad_tokens, grads = pullback((cot_out.astype(jnp.float32), cot_weight.astype(jnp.float32)))
    return (layer_out.astype(jnp.bfloat16), term_weight, grad_tokens, grads[0], grads[1], grads[2], grads[3], grads[4], grads[5], grads[6], grads[7], grads[8], grads[9], grads[10], grads[11], grads[12], grads[13], grads[14], grads[15])
```

```python
from functools import partial

import jax
import jax.numpy as jnp
from jax import lax
from jax.experimental import pallas as pl
from jax.experimental.pallas import tpu as pltpu
from jax.sharding import PartitionSpec as P

HD = 64
EPS = 1e-06
MASKED = -1e30
bf16 = jnp.bfloat16
f32 = jnp.float32
AXES = ("batch", "seq")
PAIR = 2 * HD
VMEM = pl.BlockSpec(memory_space=pltpu.VMEM)
SMEM = pl.BlockSpec(memory_space=pltpu.SMEM)
HBM = pl.BlockSpec(memory_space=pl.ANY)


def dot(left, right, left_dim=1, right_dim=0):
    dims = (((left_dim,), (right_dim,)), ((), ()))
    return lax.dot_general(left, right, dims, preferred_element_type=f32)


def fetch(source, target, sem):
    copy = pltpu.make_async_copy(source, target, sem)
    copy.start()
    return copy


def column(row):
    return jnp.transpose(jnp.broadcast_to(row, (128, row.shape[1])))[:, :1]


def row_of(col):
    return jnp.transpose(jnp.broadcast_to(col, (col.shape[0], 128)))[:1]


def half_masks():
    lane = lax.broadcasted_iota(jnp.int32, (1, PAIR), 1)
    low = (lane < HD).astype(f32)
    return low.astype(bf16), (1.0 - low).astype(bf16)


def store_blocks(out, at, group, values, flip, rows):
    per = values.shape[0] // rows
    for i in range(per):
        place = (group * per + i) ^ flip
        start = pl.multiple_of(place * rows, 16)
        out[at, pl.ds(start, rows), :] = values[i * rows : (i + 1) * rows]


def project_kernel(x, wq, bq, wk, wv, bv, q, k, v):
    t = x[...]
    q[...] = (dot(t, wq[...]) + bq[...]).astype(bf16) * bf16(HD**-0.5)
    k[...] = dot(t, wk[...]).astype(bf16)
    v[...] = (dot(t, wv[...]) + bv[...]).astype(bf16)


def norm_forward(values):
    centered = values - jnp.mean(values, -1, keepdims=True)
    inverse = lax.rsqrt(jnp.mean(centered * centered, -1, keepdims=True) + EPS)
    return centered * inverse, inverse


def norm_backward(grad, gain, normed, inverse):
    g = grad * gain
    return inverse * (
        g - jnp.mean(g, -1, keepdims=True) - normed * jnp.mean(g * normed, -1, keepdims=True)
    )


def forward_kernel(
    scal, x_own, x_oth, q, k_own, v_own, seg, bv, b_out, gain1, shift1, b_up, b_down,
    gain2, shift2, w_head, cot, cot_weight, wk_h, wv_h, w_out_h, w_up_h, w_down_h,
    layer_out, term, probs_h, k_all, v_all, att_t, normed1, inv1, first_low, slope,
    grad_sum2, grad_down, vecs, send_h, keep_h,
    wk, wv, w_out, w_up, w_down, v_t, probs, active, packed, w_sems, p_sems, o_sems,
):
    loads = [
        fetch(a, b, w_sems.at[n])
        for n, (a, b) in enumerate(
            ((wk_h, wk), (wv_h, wv), (w_out_h, w_out), (w_up_h, w_up), (w_down_h, w_down))
        )
    ]
    here, width = x_own.shape
    half, core, flip_keep, flip_send = scal[0], scal[1], scal[2], scal[3]
    heads = width // HD
    loads[0].wait()
    loads[1].wait()
    other = x_oth[...]
    k_all[:here] = k_own[...]
    v_all[:here] = v_own[...]
    k_all[here:] = dot(other, wk[...]).astype(bf16)
    v_all[here:] = (dot(other, wv[...]) + bv[...]).astype(bf16)
    v_t[...] = jnp.transpose(v_all[...])

    own_ids = seg[:, pl.ds(pl.multiple_of(half * here, 128), here)].astype(f32)
    oth_ids = seg[:, pl.ds(pl.multiple_of((1 - half) * here, 128), here)].astype(f32)
    key_ids = jnp.concatenate([own_ids, oth_ids], 1)
    bias = jnp.where(column(key_ids) == own_ids, 0.0, MASKED)
    masks = half_masks()
    stores = []
    for p in range(heads // 2):
        lanes = slice(p * PAIR, (p + 1) * PAIR)
        q_pair, k_pair = q[:, lanes], k_all[:, lanes]
        for e in range(2):
            h = 2 * p + e
            scores = dot(k_pair, q_pair * masks[e], 1, 1) + bias
            weights = jnp.exp(scores - jnp.max(scores, 0, keepdims=True))
            weights = weights * (1.0 / jnp.sum(weights, 0, keepdims=True))
            low = weights.astype(bf16)
            probs[h] = low
            att_t[h * HD : (h + 1) * HD] = dot(v_t[h * HD : (h + 1) * HD], low).astype(bf16)
        stores.append(fetch(probs.at[pl.ds(2 * p, 2)], probs_h.at[pl.ds(2 * p, 2)], p_sems.at[p]))

    loads[2].wait()
    attn_out = dot(att_t[...], w_out[...], 0, 0) + b_out[...]
    n1, i1 = norm_forward(x_own[...].astype(f32) + attn_out)
    normed1[...] = n1
    inv1[...] = jnp.broadcast_to(i1, inv1.shape)
    first = n1 * gain1[...] + shift1[...]
    f_low = first.astype(bf16)
    first_low[...] = f_low

    loads[3].wait()
    loads[4].wait()
    down = first + b_down[...]
    chunk = 512
    for j in range(w_up.shape[1] // chunk):
        cols = slice(j * chunk, (j + 1) * chunk)
        u = dot(f_low, w_up[:, cols]) + b_up[:, cols]
        cdf = 0.5 + 0.5 * lax.erf(u * (2.0**-0.5))
        pdf = jnp.exp(-0.5 * u * u) * 0.3989422804014327
        slope[:, cols] = (cdf + u * pdf).astype(bf16)
        act = (u * cdf).astype(bf16)
        active[:, cols] = act
        down = down + dot(act, w_down[cols, :])

    n2, i2 = norm_forward(down)
    second = n2 * gain2[...] + shift2[...]
    layer_out[...] = second.astype(bf16)
    head = w_head[...].astype(f32)
    logits = jnp.sum(second * head, -1, keepdims=True)
    softplus = jnp.maximum(logits, 0.0) + jnp.log1p(jnp.exp(-jnp.abs(logits)))
    term[...] = row_of(softplus)
    grad_logits = column(cot_weight[...]) * lax.logistic(logits)
    vecs[0:1] = jnp.sum(grad_logits * second, 0, keepdims=True)
    grad_second = cot[...].astype(f32) + grad_logits * head
    vecs[1:2] = jnp.sum(grad_second * n2, 0, keepdims=True)
    vecs[2:3] = jnp.sum(grad_second, 0, keepdims=True)
    g_sum2 = norm_backward(grad_second, gain2[...], n2, i2)
    grad_sum2[...] = g_sum2
    g_down = g_sum2.astype(bf16)
    grad_down[...] = g_down
    vecs[3:4] = jnp.sum(g_down.astype(f32), 0, keepdims=True)
    vecs[4:8] = jnp.zeros((4, width), f32)

    rows = packed.shape[1] // 16
    outs = []
    for e, (which, flip, out) in enumerate(
        ((1 - core, flip_send, send_h), (core, flip_keep, keep_h))
    ):
        for j in range(2):
            start = pl.multiple_of((which * 2 + j) * width, 128)
            grad = dot(active[:, pl.ds(start, width)], g_down, 0, 0).astype(bf16)
            store_blocks(packed, e, j, grad, flip, rows)
        outs.append(fetch(packed.at[e], out, o_sems.at[e]))
    for copy in stores + outs:
        copy.wait()


def upper_kernel(
    scal, first_low, slope, grad_down, w_down_h, grad_upper, vecs, send_h, keep_h,
    w_down, packed, w_sems, o_sems,
):
    here, width = first_low.shape
    core, flip_keep, flip_send = scal[1], scal[4], scal[5]
    order = [(e, w, j) for e, w in enumerate((1 - core, core)) for j in range(2)]
    loads = []
    for n, (e, which, j) in enumerate(order):
        part = pl.ds(pl.multiple_of((which * 2 + j) * width, 16), width)
        loads.append(fetch(w_down_h.at[part, :], w_down.at[n], w_sems.at[n]))
    first_t = jnp.transpose(first_low[...])
    g_down = grad_down[...]
    rows = packed.shape[1] // 16
    outs = []
    for n, (e, which, j) in enumerate(order):
        start = pl.multiple_of((which * 2 + j) * width, 128)
        loads[n].wait()
        g_active = dot(g_down, w_down[n], 1, 1)
        g_upper = (g_active * slope[:, pl.ds(start, width)].astype(f32)).astype(bf16)
        grad_upper[:, pl.ds(start, width)] = g_upper
        vecs[pl.ds(which * 2 + j, 1), :] = jnp.sum(g_upper.astype(f32), 0, keepdims=True)
        grad = dot(first_t, g_upper).astype(bf16)
        store_blocks(packed, e, j, grad, (flip_send, flip_keep)[e], rows)
        if j == 1:
            outs.append(fetch(packed.at[e], (send_h, keep_h)[e], o_sems.at[e]))
    vecs[4:8] = jnp.zeros((4, width), f32)
    for copy in outs:
        copy.wait()


def first_back_kernel(
    grad_sum2, grad_upper, normed1, inv1, gain1, w_up_h, w_out_h,
    grad_sum1, grad_attn, grad_mix, vecs, w_up, w_out, sems,
):
    load_up = fetch(w_up_h, w_up, sems.at[0])
    load_out = fetch(w_out_h, w_out, sems.at[1])
    n1 = normed1[...]
    load_up.wait()
    grad_first = grad_sum2[...] + dot(grad_upper[...], w_up[...], 1, 1)
    vecs[0:1] = jnp.sum(grad_first * n1, 0, keepdims=True)
    vecs[1:2] = jnp.sum(grad_first, 0, keepdims=True)
    g_sum1 = norm_backward(grad_first, gain1[...], n1, inv1[:, :1])
    grad_sum1[...] = g_sum1
    g_attn = g_sum1.astype(bf16)
    grad_attn[...] = g_attn
    vecs[2:3] = jnp.sum(g_attn.astype(f32), 0, keepdims=True)
    vecs[3:8] = jnp.zeros((5, vecs.shape[1]), f32)
    load_out.wait()
    grad_mix[...] = dot(g_attn, w_out[...], 1, 1).astype(bf16)


def attention_back_kernel(
    scal, x_own, x_oth, q, k_all, v_all, probs_h, att_t, grad_attn, grad_mix, vec_a, vec_b, vec_c,
    grad_query, grad_key, grad_value, extra, send_h, keep_h,
    probs, k_t, x_t, gq_t, vec_all, packed, p_sems, o_sems,
):
    here, width = x_own.shape
    heads = width // HD
    core, flip_keep, flip_send = scal[1], scal[2], scal[3]
    loads = [
        fetch(probs_h.at[pl.ds(2 * p, 2)], probs.at[pl.ds(2 * p, 2)], p_sems.at[p])
        for p in range(heads // 2)
    ]
    k_t[...] = jnp.transpose(k_all[...])
    masks = half_masks()
    for p in range(heads // 2):
        lanes = slice(p * PAIR, (p + 1) * PAIR)
        mix_pair, q_pair, v_pair = grad_mix[:, lanes], q[:, lanes], v_all[:, lanes]
        mixes = [mix_pair * m for m in masks]
        queries = [q_pair * m for m in masks]
        loads[p].wait()
        grads = []
        for e in range(2):
            h = 2 * p + e
            weights = probs[h].astype(f32)
            product = weights * dot(v_pair, mixes[e], 1, 1)
            delta = jnp.sum(product, 0, keepdims=True)
            grad_scores = (product - weights * delta).astype(bf16)
            grads.append(grad_scores)
            gq_t[h * HD : (h + 1) * HD] = (
                dot(k_t[h * HD : (h + 1) * HD], grad_scores) * (HD**-0.5)
            ).astype(bf16)
        both = jnp.concatenate([probs[2 * p], probs[2 * p + 1]], 1)
        grad_value[:, lanes] = dot(both, jnp.concatenate(mixes, 0)).astype(bf16)
        grad_key[:, lanes] = dot(
            jnp.concatenate(grads, 1), jnp.concatenate(queries, 0)
        ).astype(bf16)
    g_query = jnp.transpose(gq_t[...])
    grad_query[...] = g_query
    x_t[:, :here] = jnp.transpose(x_own[...])
    x_t[:, here:] = jnp.transpose(x_oth[...])

    vec_all[0:8] = vec_a[...]
    vec_all[4:8] = vec_b[0:4]
    vec_all[8:16] = vec_c[...]
    vec_all[11:12] = jnp.sum(g_query.astype(f32), 0, keepdims=True)
    vec_all[12:13] = jnp.sum(grad_value[...].astype(f32), 0, keepdims=True)
    extra_low = vec_all[...].astype(bf16)
    extra[...] = extra_low

    total = packed.shape[1] - 16
    rows = total // 16
    packed[0, total:] = extra_low
    packed[1, total:] = extra_low
    for n in range(4):
        if n == 0:
            grad = dot(x_t[:, :here], gq_t[...], 1, 1)
        elif n == 1:
            grad = dot(att_t[...], grad_attn[...])
        elif n == 2:
            grad = dot(x_t[...], grad_key[...])
        else:
            grad = dot(x_t[...], grad_value[...])
        keeps = (core == n // 2).astype(jnp.int32)
        flip = jnp.where(core == n // 2, flip_keep, flip_send)
        store_blocks(packed, keeps, n % 2, grad.astype(bf16), flip, rows)
    outs = [
        fetch(packed.at[0], send_h, o_sems.at[0]),
        fetch(packed.at[1, pl.ds(0, total)], keep_h, o_sems.at[1]),
    ]
    for copy in outs:
        copy.wait()


def tokens_kernel(grad_sum1, grad_query, grad_key, grad_value, wq, wk, wv, own, other):
    here = grad_sum1.shape[0]
    w_key, w_value = wk[...], wv[...]
    other[...] = (
        dot(grad_key[here:], w_key, 1, 1) + dot(grad_value[here:], w_value, 1, 1)
    ).astype(bf16)
    own[...] = (
        grad_sum1[...]
        + dot(grad_query[...], wq[...], 1, 1)
        + dot(grad_key[:here], w_key, 1, 1)
        + dot(grad_value[:here], w_value, 1, 1)
    )


def unpack_kernel(kind, flips, scal, own, received, *refs):
    outs, (scratch, sems) = refs[:-2], refs[-2:]
    core = scal[1]
    width = own.shape[1]
    rows = own.shape[0] // 16
    per = width // rows
    for e, source in enumerate((own, received)):
        which = core if e == 0 else 1 - core
        flip = scal[flips[e]]
        for j in range(2):
            for i in range(per):
                place = pl.multiple_of(((j * per + i) ^ flip) * rows, 16)
                scratch[2 * e + j, i * rows : (i + 1) * rows, :] = source[
                    pl.ds(place, rows), :
                ].astype(f32)
            part = scratch.at[2 * e + j]
            sem = sems.at[2 * e + j]
            start = pl.multiple_of((which * 2 + j) * width, 128)
            if kind == "rows":
                fetch(part, outs[0].at[pl.ds(start, width), :], sem)
            elif kind == "columns":
                fetch(part, outs[0].at[:, pl.ds(start, width)], sem)
            else:
                for group in range(2):
                    @pl.when(which == group)
                    def _():
                        fetch(part, outs[2 * group + j], sem)
    for n in range(4):
        part = scratch.at[n]
        pltpu.make_async_copy(part, part, sems.at[n]).wait()


def call(kernel, in_specs, out_shapes, out_specs, scratch, flops, moved, exps=0):
    return pl.pallas_call(
        kernel,
        in_specs=in_specs,
        out_shape=out_shapes,
        out_specs=out_specs,
        scratch_shapes=scratch,
        compiler_params=pltpu.CompilerParams(vmem_limit_bytes=56 * 2**20),
        cost_estimate=pl.CostEstimate(
            flops=int(flops), bytes_accessed=int(moved), transcendentals=int(exps)
        ),
    )


CORE, NEAR, SEQ = 1, 2, 0


def orders(bits, first):
    rest = list(range(3, bits))
    if first == "plane":
        pairs = [(NEAR, SEQ), (SEQ, NEAR), (rest[0], rest[0]), (rest[1], rest[1])]
    else:
        pairs = [(rest[0], rest[0]), (NEAR, SEQ), (SEQ, NEAR), (rest[1], rest[1])]
    return pairs, [(b, b) for b in rest[2:]]


def flip_of(index, pairs, core):
    bits = [(index >> pair[core]) & 1 for pair in pairs]
    return sum(b << (len(pairs) - 1 - n) for n, b in enumerate(bits))


def swap(values, pair, count):
    perm = [(i, i ^ (1 << pair[(i >> CORE) & 1])) for i in range(count)]
    return lax.ppermute(values, AXES, perm)


def scatter_sum(keep, send, pairs, more, count, extra=None):
    for pair in [(CORE, CORE)] + pairs:
        size = keep.shape[0]
        got = swap(send, pair, count)
        if extra is not None:
            extra = extra + got[size:]
        if size > keep.shape[0] // 2 and pair is not pairs[-1]:
            half = size // 2
            total_keep = keep[:half] + got[:half]
            send = keep[half:] + got[half:size]
            keep = total_keep
            if extra is not None:
                send = jnp.concatenate([send, extra], 0)
        else:
            keep = keep + got[:size]
    if more:
        if extra is not None:
            keep = jnp.concatenate([keep, extra], 0)
        for pair in more:
            keep = keep + swap(keep, pair, count)
        if extra is not None:
            keep, extra = keep[:-16], keep[-16:]
    return keep, extra


def gather_all(part, pairs, count):
    for pair in reversed(pairs):
        part = jnp.concatenate([part, swap(part, pair, count)], 0)
    return part, swap(part, (CORE, CORE), count)


def body(
    count, tokens, segment_ids, w_query, b_query, w_key, w_value, b_value, w_out, b_out,
    gain_attn, shift_attn, w_up, b_up, w_down, b_down, gain_ffn, shift_ffn, w_head, cot_out,
    cot_weight,
):
    row_count, here, width = tokens.shape
    hidden = w_up.shape[1]
    heads = width // HD
    keys = segment_ids.shape[1]
    bits = count.bit_length() - 1
    share = hidden // 2
    rows = share // 16

    seq = lax.axis_index("seq")
    index = lax.axis_index("batch") * 2 + seq
    core = (index >> CORE) & 1
    plane, more = orders(bits, "plane")
    line, _ = orders(bits, "line")
    scal = [seq, core]
    for pairs in (plane, line):
        flips = [flip_of(index, pairs, c) for c in (0, 1)]
        scal.append(jnp.where(core == 0, flips[0], flips[1]))
        scal.append(jnp.where(core == 0, flips[1], flips[0]))
    scal = jnp.stack([jnp.asarray(v, jnp.int32) for v in scal])

    x_own = tokens.reshape(here, width)
    x_oth = lax.ppermute(x_own, "seq", [(0, 1), (1, 0)])
    line_of = lambda v: v.reshape(1, -1)
    sds = jax.ShapeDtypeStruct
    dma = pltpu.SemaphoreType.DMA

    q, k_own, v_own = call(
        project_kernel,
        [VMEM] * 6,
        [sds((here, width), bf16)] * 3,
        [VMEM] * 3,
        [],
        6 * here * width * width,
        3.6e6 + 1.6e6,
    )(x_own, w_query, line_of(b_query), w_key, w_value, line_of(b_value))

    packed_shape = [sds((share, width), bf16)] * 2
    (
        layer_out, term, probs, k_all, v_all, att_t, normed1, inv1, first_low, slope,
        grad_sum2, grad_down, vec_a, send_d, keep_d,
    ) = call(
        forward_kernel,
        [SMEM] + [VMEM] * 17 + [HBM] * 5,
        [
            sds((here, width), bf16),
            sds((1, here), f32),
            sds((heads, keys, here), bf16),
            sds((keys, width), bf16),
            sds((keys, width), bf16),
            sds((width, here), bf16),
            sds((here, width), f32),
            sds((here, 128), f32),
            sds((here, width), bf16),
            sds((here, hidden), bf16),
            sds((here, width), f32),
            sds((here, width), bf16),
            sds((8, width), f32),
        ]
        + packed_shape,
        [VMEM, VMEM, HBM] + [VMEM] * 10 + [HBM, HBM],
        [
            pltpu.VMEM((width, width), bf16),
            pltpu.VMEM((width, width), bf16),
            pltpu.VMEM((width, width), bf16),
            pltpu.VMEM((width, hidden), bf16),
            pltpu.VMEM((hidden, width), bf16),
            pltpu.VMEM((width, keys), bf16),
            pltpu.VMEM((heads, keys, here), bf16),
            pltpu.VMEM((here, hidden), bf16),
            pltpu.VMEM((2, share, width), bf16),
            dma((5,)),
            dma((heads // 2,)),
            dma((2,)),
        ],
        2 * here * width * (3 * width + 3 * hidden) + 4 * heads * keys * here * 128,
        30e6,
        heads * keys * here + 2 * here * hidden,
    )(
        scal, x_own, x_oth, q, k_own, v_own, segment_ids, line_of(b_value), line_of(b_out),
        line_of(gain_attn), line_of(shift_attn), line_of(b_up), line_of(b_down),
        line_of(gain_ffn), line_of(shift_ffn), line_of(w_head), cot_out.reshape(here, width),
        cot_weight, w_key, w_value, w_out, w_up, w_down,
    )
    part_d, _ = scatter_sum(keep_d, send_d, plane, more, count)

    grad_upper, vec_b, send_u, keep_u = call(
        upper_kernel,
        [SMEM] + [VMEM] * 3 + [HBM],
        [sds((here, hidden), bf16), sds((8, width), f32)] + packed_shape,
        [VMEM, VMEM, HBM, HBM],
        [
            pltpu.VMEM((4, width, width), bf16),
            pltpu.VMEM((2, share, width), bf16),
            dma((4,)),
            dma((2,)),
        ],
        4 * here * width * hidden,
        15e6,
    )(scal, first_low, slope, grad_down, w_down)
    part_u, _ = scatter_sum(keep_u, send_u, line, more, count)

    grad_sum1, grad_attn, grad_mix, vec_c = call(
        first_back_kernel,
        [VMEM] * 5 + [HBM] * 2,
        [
            sds((here, width), f32),
            sds((here, width), bf16),
            sds((here, width), bf16),
            sds((8, width), f32),
        ],
        [VMEM] * 4,
        [pltpu.VMEM((width, hidden), bf16), pltpu.VMEM((width, width), bf16), dma((2,))],
        2 * here * width * (hidden + width),
        12e6,
    )(grad_sum2, grad_upper, normed1, inv1, line_of(gain_attn), w_up, w_out)

    grad_query, grad_key, grad_value, extra, send_q, keep_q = call(
        attention_back_kernel,
        [SMEM] + [VMEM] * 5 + [HBM] + [VMEM] * 6,
        [
            sds((here, width), bf16),
            sds((keys, width), bf16),
            sds((keys, width), bf16),
            sds((16, width), bf16),
            sds((share + 16, width), bf16),
            sds((share, width), bf16),
        ],
        [VMEM] * 4 + [HBM] * 2,
        [
            pltpu.VMEM((heads, keys, here), bf16),
            pltpu.VMEM((width, keys), bf16),
            pltpu.VMEM((width, keys), bf16),
            pltpu.VMEM((width, here), bf16),
            pltpu.VMEM((16, width), f32),
            pltpu.VMEM((2, share + 16, width), bf16),
            dma((heads // 2,)),
            dma((2,)),
        ],
        12 * here * width * width + 8 * heads * keys * here * 128,
        15e6,
    )(
        scal, x_own, x_oth, q, k_all, v_all, probs, att_t, grad_attn, grad_mix,
        vec_a, vec_b, vec_c,
    )
    part_q, extra = scatter_sum(keep_q, send_q, plane, more, count, extra)

    own, other = call(
        tokens_kernel,
        [VMEM] * 7,
        [sds((here, width), f32), sds((here, width), bf16)],
        [VMEM] * 2,
        [],
        10 * here * width * width,
        7e6,
    )(grad_sum1, grad_query, grad_key, grad_value, w_query, w_key, w_value)
    grad_tokens = own + lax.ppermute(other, "seq", [(0, 1), (1, 0)]).astype(f32)

    def unpack(kind, flips, part, pairs, shapes):
        own_half, other_half = gather_all(part, pairs, count)
        return call(
            partial(unpack_kernel, kind, flips),
            [SMEM, VMEM, VMEM],
            [sds(s, f32) for s in shapes],
            [HBM] * len(shapes),
            [pltpu.VMEM((4, width, width), f32), dma((4,))],
            0,
            14e6,
        )(scal, own_half, other_half)

    (grad_w_down,) = unpack("rows", (2, 3), part_d, plane, [(hidden, width)])
    (grad_w_up,) = unpack("columns", (4, 5), part_u, line, [(width, hidden)])
    grad_w_query, grad_w_out, grad_w_key, grad_w_value = unpack(
        "groups", (2, 3), part_q, plane, [(width, width)] * 4
    )
    vec = extra.astype(f32)
    return (
        layer_out.reshape(row_count, here, width),
        term.reshape(row_count, here),
        grad_tokens.reshape(row_count, here, width),
        grad_w_query,
        vec[11],
        grad_w_key,
        grad_w_value,
        vec[12],
        grad_w_out,
        vec[10],
        vec[8],
        vec[9],
        grad_w_up,
        vec[4:8].reshape(-1),
        grad_w_down,
        vec[3],
        vec[1],
        vec[2],
        vec[0],
    )


def solution(mesh):
    rows, places = P("batch", "seq", None), P("batch", "seq")
    in_specs = (rows, P("batch", None)) + (P(),) * 16 + (rows, places)
    out_specs = (rows, places, rows) + (P(),) * 16
    count = mesh.shape["batch"] * mesh.shape["seq"]
    return jax.shard_map(
        partial(body, count), mesh=mesh, in_specs=in_specs, out_specs=out_specs, check_vma=False
    )
```

```python
from functools import partial

import jax
import jax.numpy as jnp
from jax import lax
from jax.experimental import pallas as pl
from jax.experimental.pallas import tpu as pltpu
from jax.sharding import PartitionSpec as P

HD = 64
EPS = 1e-06
MASKED = -1e30
bf16 = jnp.bfloat16
f32 = jnp.float32
AXES = ("batch", "seq")
PAIR = 2 * HD
VMEM = pl.BlockSpec(memory_space=pltpu.VMEM)
SMEM = pl.BlockSpec(memory_space=pltpu.SMEM)
HBM = pl.BlockSpec(memory_space=pl.ANY)


def dot(left, right, left_dim=1, right_dim=0):
    dims = (((left_dim,), (right_dim,)), ((), ()))
    return lax.dot_general(left, right, dims, preferred_element_type=f32)


def fetch(source, target, sem):
    copy = pltpu.make_async_copy(source, target, sem)
    copy.start()
    return copy


def column(row):
    return jnp.transpose(jnp.broadcast_to(row, (128, row.shape[1])))[:, :1]


def row_of(col):
    return jnp.transpose(jnp.broadcast_to(col, (col.shape[0], 128)))[:1]


def line(ref, part=slice(None)):
    return ref[part].reshape(1, -1)


def half_masks():
    lane = lax.broadcasted_iota(jnp.int32, (1, PAIR), 1)
    low = (lane < HD).astype(f32)
    return low.astype(bf16), (1.0 - low).astype(bf16)


def store_blocks(out, at, group, values, flip, rows):
    per = values.shape[0] // rows
    for i in range(per):
        place = (group * per + i) ^ flip
        start = pl.multiple_of(place * rows, 16)
        out[at, pl.ds(start, rows), :] = values[i * rows : (i + 1) * rows]


def project_kernel(x, wq, bq, wk, wv, bv, q, k, v):
    t = x[...]
    q[...] = (dot(t, wq[...]) + line(bq)).astype(bf16) * bf16(HD**-0.5)
    k[...] = dot(t, wk[...]).astype(bf16)
    v[...] = (dot(t, wv[...]) + line(bv)).astype(bf16)


def norm_forward(values):
    centered = values - jnp.mean(values, -1, keepdims=True)
    inverse = lax.rsqrt(jnp.mean(centered * centered, -1, keepdims=True) + EPS)
    return centered * inverse, inverse


def norm_backward(grad, gain, normed, inverse):
    g = grad * gain
    return inverse * (
        g - jnp.mean(g, -1, keepdims=True) - normed * jnp.mean(g * normed, -1, keepdims=True)
    )


def forward_kernel(
    scal, x_own, x_oth, q, k_own, v_own, seg, bv, b_out, gain1, shift1, b_up, b_down,
    gain2, shift2, w_head, cot, cot_weight, wk_h, wv_h, w_out_h, w_up_h, w_down_h,
    layer_out, term, probs_h, k_all, v_all, att_t, normed1, inv1, first_low, slope,
    grad_sum2, grad_down, vecs, send_h, keep_h,
    wk, wv, w_out, w_up, w_down, v_t, probs, active, packed, w_sems, p_sems, o_sems,
):
    loads = [
        fetch(a, b, w_sems.at[n])
        for n, (a, b) in enumerate(
            ((wk_h, wk), (wv_h, wv), (w_out_h, w_out), (w_up_h, w_up), (w_down_h, w_down))
        )
    ]
    here, width = x_own.shape
    half, core, flip_keep, flip_send = scal[0], scal[1], scal[2], scal[3]
    heads = width // HD
    loads[0].wait()
    loads[1].wait()
    other = x_oth[...]
    k_all[:here] = k_own[...]
    v_all[:here] = v_own[...]
    k_all[here:] = dot(other, wk[...]).astype(bf16)
    v_all[here:] = (dot(other, wv[...]) + line(bv)).astype(bf16)
    v_t[...] = jnp.transpose(v_all[...])

    own_ids = seg[:, pl.ds(pl.multiple_of(half * here, 128), here)].astype(f32)
    oth_ids = seg[:, pl.ds(pl.multiple_of((1 - half) * here, 128), here)].astype(f32)
    key_ids = jnp.concatenate([own_ids, oth_ids], 1)
    bias = jnp.where(column(key_ids) == own_ids, 0.0, MASKED)
    masks = half_masks()
    stores = []
    for p in range(heads // 2):
        lanes = slice(p * PAIR, (p + 1) * PAIR)
        q_pair, k_pair = q[:, lanes], k_all[:, lanes]
        for e in range(2):
            h = 2 * p + e
            scores = dot(k_pair, q_pair * masks[e], 1, 1) + bias
            weights = jnp.exp(scores - jnp.max(scores, 0, keepdims=True))
            weights = weights * (1.0 / jnp.sum(weights, 0, keepdims=True))
            low = weights.astype(bf16)
            probs[h] = low
            att_t[h * HD : (h + 1) * HD] = dot(v_t[h * HD : (h + 1) * HD], low).astype(bf16)
        stores.append(fetch(probs.at[pl.ds(2 * p, 2)], probs_h.at[pl.ds(2 * p, 2)], p_sems.at[p]))

    loads[2].wait()
    attn_out = dot(att_t[...], w_out[...], 0, 0) + line(b_out)
    n1, i1 = norm_forward(x_own[...].astype(f32) + attn_out)
    normed1[...] = n1
    inv1[...] = jnp.broadcast_to(i1, inv1.shape)
    first = n1 * line(gain1) + line(shift1)
    f_low = first.astype(bf16)
    first_low[...] = f_low

    loads[3].wait()
    loads[4].wait()
    down = first + line(b_down)
    chunk = 512
    for j in range(w_up.shape[1] // chunk):
        cols = slice(j * chunk, (j + 1) * chunk)
        u = dot(f_low, w_up[:, cols]) + line(b_up, cols)
        cdf = 0.5 + 0.5 * lax.erf(u * (2.0**-0.5))
        pdf = jnp.exp(-0.5 * u * u) * 0.3989422804014327
        slope[:, cols] = (cdf + u * pdf).astype(bf16)
        act = (u * cdf).astype(bf16)
        active[:, cols] = act
        down = down + dot(act, w_down[cols, :])

    n2, i2 = norm_forward(down)
    second = n2 * line(gain2) + line(shift2)
    layer_out[...] = second.astype(bf16)
    head = line(w_head).astype(f32)
    logits = jnp.sum(second * head, -1, keepdims=True)
    softplus = jnp.maximum(logits, 0.0) + jnp.log1p(jnp.exp(-jnp.abs(logits)))
    term[...] = row_of(softplus)
    grad_logits = column(cot_weight[...]) * lax.logistic(logits)
    vecs[0:1] = jnp.sum(grad_logits * second, 0, keepdims=True)
    grad_second = cot[...].astype(f32) + grad_logits * head
    vecs[1:2] = jnp.sum(grad_second * n2, 0, keepdims=True)
    vecs[2:3] = jnp.sum(grad_second, 0, keepdims=True)
    g_sum2 = norm_backward(grad_second, line(gain2), n2, i2)
    grad_sum2[...] = g_sum2
    g_down = g_sum2.astype(bf16)
    grad_down[...] = g_down
    vecs[3:4] = jnp.sum(g_down.astype(f32), 0, keepdims=True)
    vecs[4:8] = jnp.zeros((4, width), f32)

    rows = packed.shape[1] // BLOCKS
    outs = []
    for e, (which, flip, out) in enumerate(
        ((1 - core, flip_send, send_h), (core, flip_keep, keep_h))
    ):
        for j in range(2):
            start = pl.multiple_of((which * 2 + j) * width, 128)
            grad = dot(active[:, pl.ds(start, width)], g_down, 0, 0).astype(bf16)
            store_blocks(packed, e, j, grad, flip, rows)
        outs.append(fetch(packed.at[e], out, o_sems.at[e]))
    for copy in stores + outs:
        copy.wait()


def upper_kernel(
    scal, first_low, slope, grad_down, w_down_h, after, grad_upper, vecs, send_h, keep_h,
    w_down, packed, w_sems, o_sems,
):
    here, width = first_low.shape
    core, flip_keep, flip_send = scal[1], scal[4], scal[5]
    order = [(e, w, j) for e, w in enumerate((1 - core, core)) for j in range(2)]
    loads = []
    for n, (e, which, j) in enumerate(order):
        part = pl.ds(pl.multiple_of((which * 2 + j) * width, 16), width)
        loads.append(fetch(w_down_h.at[part, :], w_down.at[n], w_sems.at[n]))
    first_t = jnp.transpose(first_low[...])
    g_down = grad_down[...]
    rows = packed.shape[1] // BLOCKS
    outs = []
    for n, (e, which, j) in enumerate(order):
        start = pl.multiple_of((which * 2 + j) * width, 128)
        loads[n].wait()
        g_active = dot(g_down, w_down[n], 1, 1)
        g_upper = (g_active * slope[:, pl.ds(start, width)].astype(f32)).astype(bf16)
        grad_upper[:, pl.ds(start, width)] = g_upper
        vecs[pl.ds(which * 2 + j, 1), :] = jnp.sum(g_upper.astype(f32), 0, keepdims=True)
        grad = dot(first_t, g_upper).astype(bf16)
        store_blocks(packed, e, j, grad, (flip_send, flip_keep)[e], rows)
        if j == 1:
            outs.append(fetch(packed.at[e], (send_h, keep_h)[e], o_sems.at[e]))
    vecs[4:8] = jnp.zeros((4, width), f32)
    for copy in outs:
        copy.wait()


def first_back_kernel(
    grad_sum2, grad_upper, normed1, inv1, gain1, w_up_h, w_out_h, after,
    grad_sum1, grad_attn, grad_mix, vecs, w_up, w_out, sems,
):
    load_up = fetch(w_up_h, w_up, sems.at[0])
    load_out = fetch(w_out_h, w_out, sems.at[1])
    n1 = normed1[...]
    load_up.wait()
    grad_first = grad_sum2[...] + dot(grad_upper[...], w_up[...], 1, 1)
    vecs[0:1] = jnp.sum(grad_first * n1, 0, keepdims=True)
    vecs[1:2] = jnp.sum(grad_first, 0, keepdims=True)
    g_sum1 = norm_backward(grad_first, line(gain1), n1, inv1[:, :1])
    grad_sum1[...] = g_sum1
    g_attn = g_sum1.astype(bf16)
    grad_attn[...] = g_attn
    vecs[2:3] = jnp.sum(g_attn.astype(f32), 0, keepdims=True)
    vecs[3:8] = jnp.zeros((5, vecs.shape[1]), f32)
    load_out.wait()
    grad_mix[...] = dot(g_attn, w_out[...], 1, 1).astype(bf16)


def attention_back_kernel(
    q, k_all, v_all, probs_h, grad_mix, after,
    grad_query, query_t, grad_key, grad_value,
    probs, k_t, p_sems,
):
    width = q.shape[1]
    heads = width // HD
    loads = [
        fetch(probs_h.at[pl.ds(2 * p, 2)], probs.at[pl.ds(2 * p, 2)], p_sems.at[p])
        for p in range(heads // 2)
    ]
    k_t[...] = jnp.transpose(k_all[...])
    masks = half_masks()
    for p in range(heads // 2):
        lanes = slice(p * PAIR, (p + 1) * PAIR)
        mix_pair, q_pair, v_pair = grad_mix[:, lanes], q[:, lanes], v_all[:, lanes]
        mixes = [mix_pair * m for m in masks]
        queries = [q_pair * m for m in masks]
        loads[p].wait()
        grads = []
        for e in range(2):
            h = 2 * p + e
            weights = probs[h].astype(f32)
            product = weights * dot(v_pair, mixes[e], 1, 1)
            delta = jnp.sum(product, 0, keepdims=True)
            grad_scores = (product - weights * delta).astype(bf16)
            grads.append(grad_scores)
            query_t[h * HD : (h + 1) * HD] = (
                dot(k_t[h * HD : (h + 1) * HD], grad_scores) * (HD**-0.5)
            ).astype(bf16)
        both = jnp.concatenate([probs[2 * p], probs[2 * p + 1]], 1)
        grad_value[:, lanes] = dot(both, jnp.concatenate(mixes, 0)).astype(bf16)
        grad_key[:, lanes] = dot(
            jnp.concatenate(grads, 1), jnp.concatenate(queries, 0)
        ).astype(bf16)
    grad_query[...] = jnp.transpose(query_t[...])


def attention_weights_kernel(
    scal, x_own, x_oth, grad_query, query_t, grad_key, grad_value, att_t, grad_attn,
    vec_a, vec_b, vec_c, after,
    extra, send_h, keep_h,
    x_t, vec_all, packed, o_sems,
):
    here, width = x_own.shape
    core, flip_keep, flip_send = scal[1], scal[6], scal[7]
    x_t[:, :here] = jnp.transpose(x_own[...])
    x_t[:, here:] = jnp.transpose(x_oth[...])

    vec_all[0:8] = vec_a[...]
    vec_all[4:8] = vec_b[0:4]
    vec_all[8:16] = vec_c[...]
    vec_all[11:12] = jnp.sum(grad_query[...].astype(f32), 0, keepdims=True)
    vec_all[12:13] = jnp.sum(grad_value[...].astype(f32), 0, keepdims=True)
    extra_low = vec_all[...].astype(bf16)
    extra[...] = extra_low

    total = packed.shape[1] - 16
    rows = total // BLOCKS
    packed[0, total:] = extra_low
    packed[1, total:] = extra_low
    for n in range(4):
        if n == 0:
            grad = dot(x_t[:, :here], query_t[...], 1, 1)
        elif n == 1:
            grad = dot(att_t[...], grad_attn[...])
        elif n == 2:
            grad = dot(x_t[...], grad_key[...])
        else:
            grad = dot(x_t[...], grad_value[...])
        keeps = (core == n // 2).astype(jnp.int32)
        flip = jnp.where(core == n // 2, flip_keep, flip_send)
        store_blocks(packed, keeps, n % 2, grad.astype(bf16), flip, rows)
    outs = [
        fetch(packed.at[0], send_h, o_sems.at[0]),
        fetch(packed.at[1, pl.ds(0, total)], keep_h, o_sems.at[1]),
    ]
    for copy in outs:
        copy.wait()


def tokens_kernel(grad_sum1, grad_query, grad_key, grad_value, wq, wk, wv, after, own, other):
    here = grad_sum1.shape[0]
    w_key, w_value = wk[...], wv[...]
    other[...] = (
        dot(grad_key[here:], w_key, 1, 1) + dot(grad_value[here:], w_value, 1, 1)
    ).astype(bf16)
    own[...] = (
        grad_sum1[...]
        + dot(grad_query[...], wq[...], 1, 1)
        + dot(grad_key[:here], w_key, 1, 1)
        + dot(grad_value[:here], w_value, 1, 1)
    )


def unpack_kernel(kind, flips, outs_n, scal, own, received, *refs):
    outs, (scratch, sems) = refs[-2 - outs_n : -2], refs[-2:]
    core = scal[1]
    width = own.shape[1]
    rows = own.shape[0] // BLOCKS
    per = width // rows
    for e, source in enumerate((own, received)):
        which = core if e == 0 else 1 - core
        flip = scal[flips[e]]
        for j in range(2):
            for i in range(per):
                place = pl.multiple_of(((j * per + i) ^ flip) * rows, 16)
                scratch[2 * e + j, i * rows : (i + 1) * rows, :] = source[
                    pl.ds(place, rows), :
                ].astype(f32)
            part = scratch.at[2 * e + j]
            sem = sems.at[2 * e + j]
            start = pl.multiple_of((which * 2 + j) * width, 128)
            if kind == "rows":
                fetch(part, outs[0].at[pl.ds(start, width), :], sem)
            elif kind == "columns":
                fetch(part, outs[0].at[:, pl.ds(start, width)], sem)
            else:
                for group in range(2):
                    @pl.when(which == group)
                    def _():
                        fetch(part, outs[2 * group + j], sem)
    for n in range(4):
        part = scratch.at[n]
        pltpu.make_async_copy(part, part, sems.at[n]).wait()


def call(kernel, in_specs, out_shapes, out_specs, scratch, vmem):
    return pl.pallas_call(
        kernel,
        in_specs=in_specs,
        out_shape=out_shapes,
        out_specs=out_specs,
        scratch_shapes=scratch,
        compiler_params=pltpu.CompilerParams(vmem_limit_bytes=vmem * 2**20),
        cost_estimate=pl.CostEstimate(flops=0, bytes_accessed=0, transcendentals=0),
    )


SEQ, CORE, NEAR, LINE, FAR = range(5)

STEPS = (
    ((NEAR, SEQ), (LINE, NEAR), (SEQ, LINE)),
    ((SEQ, LINE), (NEAR, SEQ), (LINE, NEAR)),
    ((LINE, NEAR), (SEQ, LINE), (NEAR, SEQ)),
)
BLOCKS = 8
UPPER, FIRST, ATTENTION, WEIGHTS, LAUNCH, TOKENS, EXCHANGED = range(3, 10)
CHAINED = 10
ORDER = (
    (UPPER, CHAINED + 0, FIRST, CHAINED + 1, ATTENTION, CHAINED + 0, WEIGHTS, CHAINED + 1, CHAINED + 0)
    + (LAUNCH, TOKENS, CHAINED + 2, CHAINED + 1, CHAINED + 0)
    + (CHAINED + 2, CHAINED + 1, CHAINED + 0) * 2
    + (EXCHANGED,)
    + (CHAINED + 2, CHAINED + 1, CHAINED + 0) * 3
    + (CHAINED + 2, CHAINED + 1, CHAINED + 2, CHAINED + 2)
)


def flip_of(index, pairs, core):
    bits = [(index >> pair[core]) & 1 for pair in pairs]
    return sum(b << (len(pairs) - 1 - n) for n, b in enumerate(bits))


def swap(values, pair, count):
    perm = [(i, i ^ (1 << pair[(i >> CORE) & 1])) for i in range(count)]
    return lax.ppermute(values, AXES, perm)


def order_after(values, after):
    return lax.optimization_barrier((values, after))[0] if after else values


def halve(keep, got, extra, more_halves, after):
    size = keep.shape[0]
    keep, got = order_after((keep, got), after)
    if extra is not None:
        extra = extra + got[size:]
    if not more_halves:
        return keep + got[:size], None, extra
    half = size // 2
    send = keep[half:] + got[half:size]
    if extra is not None:
        send = jnp.concatenate([send, extra], 0)
    return keep[:half] + got[:half], send, extra


def join(part, got, after):
    part, got = order_after((part, got), after)
    return jnp.concatenate([part, got], 0)


def sum_stream(keep, send, pairs, more, count, finish, extra=None):
    steps = ((CORE, CORE),) + pairs
    for n, pair in enumerate(steps):
        got = swap(send, pair, count)
        after = yield keep
        keep, send, extra = halve(keep, got, extra, n < len(steps) - 1, after)
    size = keep.shape[0]
    for n, pair in enumerate(more):
        both = keep if extra is None else jnp.concatenate([keep, extra], 0)
        got = swap(both, pair, count)
        if n == 0:
            after = yield keep
            both, got = order_after((both, got), after)
        both = both + got
        keep, extra = both[:size], None if extra is None else both[size:]
    for pair in reversed(pairs):
        got = swap(keep, pair, count)
        after = yield keep
        keep = join(keep, got, after)
    got = swap(keep, (CORE, CORE), count)
    after = yield keep
    yield finish(keep, got, extra, after)


def body(
    count, tokens, segment_ids, w_query, b_query, w_key, w_value, b_value, w_out, b_out,
    gain_attn, shift_attn, w_up, b_up, w_down, b_down, gain_ffn, shift_ffn, w_head, cot_out,
    cot_weight,
):
    row_count, here, width = tokens.shape
    hidden = w_up.shape[1]
    heads = width // HD
    keys = segment_ids.shape[1]
    bits = count.bit_length() - 1
    share = hidden // 2

    seq = lax.axis_index("seq")
    index = lax.axis_index("batch") * 2 + seq
    core = (index >> CORE) & 1
    more = [(b, b) for b in range(FAR, bits)]
    scal = [seq, core]
    for pairs in STEPS:
        flips = [flip_of(index, pairs, c) for c in (0, 1)]
        scal.append(jnp.where(core == 0, flips[0], flips[1]))
        scal.append(jnp.where(core == 0, flips[1], flips[0]))
    scal = jnp.stack([jnp.asarray(v, jnp.int32) for v in scal])

    x_own = tokens.reshape(here, width)
    x_oth = lax.ppermute(x_own, "seq", [(0, 1), (1, 0)])
    sds = jax.ShapeDtypeStruct
    dma = pltpu.SemaphoreType.DMA

    q, k_own, v_own = call(
        project_kernel,
        [VMEM] * 6,
        [sds((here, width), bf16)] * 3,
        [VMEM] * 3,
        [],
        56,
    )(x_own, w_query, b_query, w_key, w_value, b_value)

    packed_shape = [sds((share, width), bf16)] * 2
    (
        layer_out, term, probs, k_all, v_all, att_t, normed1, inv1, first_low, slope,
        grad_sum2, grad_down, vec_a, send_d, keep_d,
    ) = call(
        forward_kernel,
        [SMEM] + [VMEM] * 17 + [HBM] * 5,
        [
            sds((here, width), bf16),
            sds((1, here), f32),
            sds((heads, keys, here), bf16),
            sds((keys, width), bf16),
            sds((keys, width), bf16),
            sds((width, here), bf16),
            sds((here, width), f32),
            sds((here, 128), f32),
            sds((here, width), bf16),
            sds((here, hidden), bf16),
            sds((here, width), f32),
            sds((here, width), bf16),
            sds((8, width), f32),
        ]
        + packed_shape,
        [VMEM, VMEM, HBM] + [VMEM] * 10 + [HBM, HBM],
        [
            pltpu.VMEM((width, width), bf16),
            pltpu.VMEM((width, width), bf16),
            pltpu.VMEM((width, width), bf16),
            pltpu.VMEM((width, hidden), bf16),
            pltpu.VMEM((hidden, width), bf16),
            pltpu.VMEM((width, keys), bf16),
            pltpu.VMEM((heads, keys, here), bf16),
            pltpu.VMEM((here, hidden), bf16),
            pltpu.VMEM((2, share, width), bf16),
            dma((5,)),
            dma((heads // 2,)),
            dma((2,)),
        ],
        56,
    )(
        scal, x_own, x_oth, q, k_own, v_own, segment_ids, b_value, b_out,
        gain_attn, shift_attn, b_up, b_down,
        gain_ffn, shift_ffn, w_head, cot_out.reshape(here, width),
        cot_weight, w_key, w_value, w_out, w_up, w_down,
    )

    def unpack(kind, flips, shapes):
        def finish(own_half, other_half, extra, after):
            outs = call(
                partial(unpack_kernel, kind, flips, len(shapes)),
                [SMEM, VMEM, VMEM] + [HBM] * len(after),
                [sds(s, f32) for s in shapes],
                [HBM] * len(shapes),
                [pltpu.VMEM((4, width, width), f32), dma((4,))],
                20,
            )(scal, own_half, other_half, *after)
            return outs, extra

        return finish

    streams = {}

    def launch(n, keep, send, kind, shapes, extra=None):
        flips = (2 + 2 * n, 3 + 2 * n)
        streams[n] = sum_stream(
            keep, send, STEPS[n], more, count, unpack(kind, flips, shapes), extra
        )
        next(streams[n])

    launch(0, keep_d, send_d, "rows", [(hidden, width)])
    done, ended = keep_d, {}
    for event in ORDER:
        if event == UPPER:
            grad_upper, vec_b, send_u, keep_u = call(
                upper_kernel,
                [SMEM] + [VMEM] * 3 + [HBM] * 2,
                [sds((here, hidden), bf16), sds((8, width), f32)] + packed_shape,
                [VMEM, VMEM, HBM, HBM],
                [
                    pltpu.VMEM((4, width, width), bf16),
                    pltpu.VMEM((2, share, width), bf16),
                    dma((4,)),
                    dma((2,)),
                ],
                24,
            )(scal, first_low, slope, grad_down, w_down, done)
            launch(1, keep_u, send_u, "columns", [(width, hidden)])
            done = grad_upper
        elif event == FIRST:
            grad_sum1, grad_attn, grad_mix, vec_c = call(
                first_back_kernel,
                [VMEM] * 5 + [HBM] * 3,
                [
                    sds((here, width), f32),
                    sds((here, width), bf16),
                    sds((here, width), bf16),
                    sds((8, width), f32),
                ],
                [VMEM] * 4,
                [pltpu.VMEM((width, hidden), bf16), pltpu.VMEM((width, width), bf16), dma((2,))],
                20,
            )(grad_sum2, grad_upper, normed1, inv1, gain_attn, w_up, w_out, done)
            done = grad_mix
        elif event == ATTENTION:
            grad_query, query_t, grad_key, grad_value = call(
                attention_back_kernel,
                [VMEM] * 3 + [HBM, VMEM, HBM],
                [
                    sds((here, width), bf16),
                    sds((width, here), bf16),
                    sds((keys, width), bf16),
                    sds((keys, width), bf16),
                ],
                [VMEM] * 4,
                [
                    pltpu.VMEM((heads, keys, here), bf16),
                    pltpu.VMEM((width, keys), bf16),
                    dma((heads // 2,)),
                ],
                20,
            )(q, k_all, v_all, probs, grad_mix, done)
            done = grad_query
        elif event == WEIGHTS:
            extra, send_q, keep_q = call(
                attention_weights_kernel,
                [SMEM] + [VMEM] * 11 + [HBM],
                [
                    sds((16, width), bf16),
                    sds((share + 16, width), bf16),
                    sds((share, width), bf16),
                ],
                [VMEM, HBM, HBM],
                [
                    pltpu.VMEM((width, keys), bf16),
                    pltpu.VMEM((16, width), f32),
                    pltpu.VMEM((2, share + 16, width), bf16),
                    dma((2,)),
                ],
                20,
            )(
                scal, x_own, x_oth, grad_query, query_t, grad_key, grad_value, att_t, grad_attn,
                vec_a, vec_b, vec_c, done,
            )
            done = extra
        elif event == LAUNCH:
            send_q = order_after(send_q, [done])
            launch(2, keep_q, send_q, "groups", [(width, width)] * 4, extra)
        elif event == TOKENS:
            own, other = call(
                tokens_kernel,
                [VMEM] * 7 + [HBM],
                [sds((here, width), f32), sds((here, width), bf16)],
                [VMEM] * 2,
                [],
                16,
            )(grad_sum1, grad_query, grad_key, grad_value, w_query, w_key, w_value, done)

            received = lax.ppermute(other, "seq", [(0, 1), (1, 0)])
            done = other
        elif event == EXCHANGED:
            grad_tokens = done = own + received.astype(f32)
        else:
            n = event % CHAINED
            done = streams[n].send([done] if event >= CHAINED else [])
            if isinstance(done, tuple):
                ended[n], done = done, done[0][0]

    (grad_w_down,), (grad_w_up,) = ended[0][0], ended[1][0]
    grad_w_query, grad_w_out, grad_w_key, grad_w_value = ended[2][0]
    vec = ended[2][1].astype(f32)
    return (
        layer_out.reshape(row_count, here, width),
        term.reshape(row_count, here),
        grad_tokens.reshape(row_count, here, width),
        grad_w_query,
        vec[11],
        grad_w_key,
        grad_w_value,
        vec[12],
        grad_w_out,
        vec[10],
        vec[8],
        vec[9],
        grad_w_up,
        vec[4:8].reshape(-1),
        grad_w_down,
        vec[3],
        vec[1],
        vec[2],
        vec[0],
    )


def solution(mesh):
    rows, places = P("batch", "seq", None), P("batch", "seq")
    in_specs = (rows, P("batch", None)) + (P(),) * 16 + (rows, places)
    out_specs = (rows, places, rows) + (P(),) * 16
    count = mesh.shape["batch"] * mesh.shape["seq"]
    return jax.shard_map(
        partial(body, count), mesh=mesh, in_specs=in_specs, out_specs=out_specs, check_vma=False
    )
```

```python
from functools import partial

import jax
import jax.numpy as jnp
from jax import lax
from jax.experimental import pallas as pl
from jax.experimental.pallas import tpu as pltpu
from jax.sharding import PartitionSpec as P

HD = 64
EPS = 1e-06
MASKED = -1e30
bf16 = jnp.bfloat16
f32 = jnp.float32
AXES = ("batch", "seq")
PAIR = 2 * HD
VMEM = pl.BlockSpec(memory_space=pltpu.VMEM)
SMEM = pl.BlockSpec(memory_space=pltpu.SMEM)
HBM = pl.BlockSpec(memory_space=pl.ANY)


def dot(left, right, left_dim=1, right_dim=0):
    dims = (((left_dim,), (right_dim,)), ((), ()))
    return lax.dot_general(left, right, dims, preferred_element_type=f32)


def fetch(source, target, sem):
    copy = pltpu.make_async_copy(source, target, sem)
    copy.start()
    return copy


def column(row):
    return jnp.transpose(jnp.broadcast_to(row, (128, row.shape[1])))[:, :1]


def row_of(col):
    return jnp.transpose(jnp.broadcast_to(col, (col.shape[0], 128)))[:1]


def line(ref, part=slice(None)):
    return ref[part].reshape(1, -1)


def half_masks():
    lane = lax.broadcasted_iota(jnp.int32, (1, PAIR), 1)
    low = (lane < HD).astype(f32)
    return low.astype(bf16), (1.0 - low).astype(bf16)


def store_blocks(out, at, group, values, flip, rows):
    per = values.shape[0] // rows
    for i in range(per):
        place = (group * per + i) ^ flip
        start = pl.multiple_of(place * rows, 16)
        out[at, pl.ds(start, rows), :] = values[i * rows : (i + 1) * rows]


def project_kernel(x, wq, bq, wk, wv, bv, q, k, v):
    t = x[...]
    q[...] = (dot(t, wq[...]) + line(bq)).astype(bf16) * bf16(HD**-0.5)
    k[...] = dot(t, wk[...]).astype(bf16)
    v[...] = (dot(t, wv[...]) + line(bv)).astype(bf16)


def norm_forward(values):
    centered = values - jnp.mean(values, -1, keepdims=True)
    inverse = lax.rsqrt(jnp.mean(centered * centered, -1, keepdims=True) + EPS)
    return centered * inverse, inverse


def norm_backward(grad, gain, normed, inverse):
    g = grad * gain
    return inverse * (
        g - jnp.mean(g, -1, keepdims=True) - normed * jnp.mean(g * normed, -1, keepdims=True)
    )


def middle_kernel(
    scal, x_own, x_oth, q, k_own, v_own, seg, bv, b_out, gain1, shift1, b_up, b_down,
    gain2, shift2, w_head, cot, cot_weight, wk_h, wv_h, w_out_h, w_up_h, w_down_h,
    layer_out, term, probs_h, k_all, v_all, att_t, grad_sum1, grad_attn, grad_mix, vecs,
    send_d, keep_d, send_u, keep_u,
    wk, wv, w_out, w_up, w_down, v_t, probs, active, slope, packed_d, packed_u,
    w_sems, p_sems, o_sems,
):
    loads = [
        fetch(a, b, w_sems.at[n])
        for n, (a, b) in enumerate(
            ((wk_h, wk), (wv_h, wv), (w_out_h, w_out), (w_up_h, w_up), (w_down_h, w_down))
        )
    ]
    here, width = x_own.shape
    half, core = scal[0], scal[1]
    heads = width // HD
    loads[0].wait()
    loads[1].wait()
    other = x_oth[...]
    k_all[:here] = k_own[...]
    v_all[:here] = v_own[...]
    k_all[here:] = dot(other, wk[...]).astype(bf16)
    v_all[here:] = (dot(other, wv[...]) + line(bv)).astype(bf16)
    v_t[...] = jnp.transpose(v_all[...])

    own_ids = seg[:, pl.ds(pl.multiple_of(half * here, 128), here)].astype(f32)
    oth_ids = seg[:, pl.ds(pl.multiple_of((1 - half) * here, 128), here)].astype(f32)
    key_ids = jnp.concatenate([own_ids, oth_ids], 1)
    bias = jnp.where(column(key_ids) == own_ids, 0.0, MASKED)
    masks = half_masks()
    stores = []
    for p in range(heads // 2):
        lanes = slice(p * PAIR, (p + 1) * PAIR)
        q_pair, k_pair = q[:, lanes], k_all[:, lanes]
        for e in range(2):
            h = 2 * p + e
            scores = dot(k_pair, q_pair * masks[e], 1, 1) + bias
            weights = jnp.exp(scores - jnp.max(scores, 0, keepdims=True))
            weights = weights * (1.0 / jnp.sum(weights, 0, keepdims=True))
            low = weights.astype(bf16)
            probs[h] = low
            att_t[h * HD : (h + 1) * HD] = dot(v_t[h * HD : (h + 1) * HD], low).astype(bf16)
        stores.append(fetch(probs.at[pl.ds(2 * p, 2)], probs_h.at[pl.ds(2 * p, 2)], p_sems.at[p]))

    loads[2].wait()
    attn_out = dot(att_t[...], w_out[...], 0, 0) + line(b_out)
    n1, i1 = norm_forward(x_own[...].astype(f32) + attn_out)
    first = n1 * line(gain1) + line(shift1)
    f_low = first.astype(bf16)

    loads[3].wait()
    loads[4].wait()
    down = first + line(b_down)
    chunk = 512
    for j in range(w_up.shape[1] // chunk):
        cols = slice(j * chunk, (j + 1) * chunk)
        u = dot(f_low, w_up[:, cols]) + line(b_up, cols)
        cdf = 0.5 + 0.5 * lax.erf(u * (2.0**-0.5))
        pdf = jnp.exp(-0.5 * u * u) * 0.3989422804014327
        slope[:, cols] = (cdf + u * pdf).astype(bf16)
        act = (u * cdf).astype(bf16)
        active[:, cols] = act
        down = down + dot(act, w_down[cols, :])

    n2, i2 = norm_forward(down)
    second = n2 * line(gain2) + line(shift2)
    layer_out[...] = second.astype(bf16)
    head = line(w_head).astype(f32)
    logits = jnp.sum(second * head, -1, keepdims=True)
    softplus = jnp.maximum(logits, 0.0) + jnp.log1p(jnp.exp(-jnp.abs(logits)))
    term[...] = row_of(softplus)
    grad_logits = column(cot_weight[...]) * lax.logistic(logits)
    vecs[0:1] = jnp.sum(grad_logits * second, 0, keepdims=True)
    grad_second = cot[...].astype(f32) + grad_logits * head
    vecs[1:2] = jnp.sum(grad_second * n2, 0, keepdims=True)
    vecs[2:3] = jnp.sum(grad_second, 0, keepdims=True)
    g_sum2 = norm_backward(grad_second, line(gain2), n2, i2)
    g_down = g_sum2.astype(bf16)
    vecs[3:4] = jnp.sum(g_down.astype(f32), 0, keepdims=True)
    vecs[11:] = jnp.zeros((5, width), f32)

    rows = packed_d.shape[1] // BLOCKS
    outs = []
    halves = (1 - core, core)
    for e, which in enumerate(halves):
        for j in range(2):
            start = pl.multiple_of((which * 2 + j) * width, 128)
            grad = dot(active[:, pl.ds(start, width)], g_down, 0, 0).astype(bf16)
            store_blocks(packed_d, e, j, grad, scal[3 - e], rows)
        outs.append(fetch(packed_d.at[e], (send_d, keep_d)[e], o_sems.at[e]))

    first_t = jnp.transpose(f_low)
    grad_first = g_sum2
    for e, which in enumerate(halves):
        for j in range(2):
            start = pl.multiple_of((which * 2 + j) * width, 128)
            part = pl.ds(start, width)
            g_active = dot(g_down, w_down[part, :], 1, 1)
            g_upper = (g_active * slope[:, part].astype(f32)).astype(bf16)
            vecs[pl.ds(4 + which * 2 + j, 1), :] = jnp.sum(g_upper.astype(f32), 0, keepdims=True)
            grad = dot(first_t, g_upper).astype(bf16)
            store_blocks(packed_u, e, j, grad, scal[5 - e], rows)
            grad_first = grad_first + dot(g_upper, w_up[:, part], 1, 1)
        outs.append(fetch(packed_u.at[e], (send_u, keep_u)[e], o_sems.at[2 + e]))

    vecs[8:9] = jnp.sum(grad_first * n1, 0, keepdims=True)
    vecs[9:10] = jnp.sum(grad_first, 0, keepdims=True)
    g_sum1 = norm_backward(grad_first, line(gain1), n1, i1)
    grad_sum1[...] = g_sum1
    g_attn = g_sum1.astype(bf16)
    grad_attn[...] = g_attn
    vecs[10:11] = jnp.sum(g_attn.astype(f32), 0, keepdims=True)
    grad_mix[...] = dot(g_attn, w_out[...], 1, 1).astype(bf16)
    for copy in stores + outs:
        copy.wait()


def attention_back_kernel(
    scal, x_own, x_oth, q, k_all, v_all, probs_h, att_t, grad_attn, grad_mix, vecs, after,
    grad_query, grad_key, grad_value, extra, send_h, keep_h,
    probs, k_t, x_t, query_t, vec_all, packed, p_sems, o_sems,
):
    here = x_own.shape[0]
    core, flip_keep, flip_send = scal[1], scal[6], scal[7]
    width = q.shape[1]
    heads = width // HD
    loads = [
        fetch(probs_h.at[pl.ds(2 * p, 2)], probs.at[pl.ds(2 * p, 2)], p_sems.at[p])
        for p in range(heads // 2)
    ]
    k_t[...] = jnp.transpose(k_all[...])
    masks = half_masks()
    for p in range(heads // 2):
        lanes = slice(p * PAIR, (p + 1) * PAIR)
        mix_pair, q_pair, v_pair = grad_mix[:, lanes], q[:, lanes], v_all[:, lanes]
        mixes = [mix_pair * m for m in masks]
        queries = [q_pair * m for m in masks]
        loads[p].wait()
        grads = []
        for e in range(2):
            h = 2 * p + e
            weights = probs[h].astype(f32)
            product = weights * dot(v_pair, mixes[e], 1, 1)
            delta = jnp.sum(product, 0, keepdims=True)
            grad_scores = (product - weights * delta).astype(bf16)
            grads.append(grad_scores)
            query_t[h * HD : (h + 1) * HD] = (
                dot(k_t[h * HD : (h + 1) * HD], grad_scores) * (HD**-0.5)
            ).astype(bf16)
        both = jnp.concatenate([probs[2 * p], probs[2 * p + 1]], 1)
        grad_value[:, lanes] = dot(both, jnp.concatenate(mixes, 0)).astype(bf16)
        grad_key[:, lanes] = dot(
            jnp.concatenate(grads, 1), jnp.concatenate(queries, 0)
        ).astype(bf16)
    grad_query[...] = jnp.transpose(query_t[...])
    x_t[:, :here] = jnp.transpose(x_own[...])
    x_t[:, here:] = jnp.transpose(x_oth[...])

    vec_all[...] = vecs[...]
    vec_all[11:12] = jnp.sum(grad_query[...].astype(f32), 0, keepdims=True)
    vec_all[12:13] = jnp.sum(grad_value[...].astype(f32), 0, keepdims=True)
    extra_low = vec_all[...].astype(bf16)
    extra[...] = extra_low

    total = packed.shape[1] - 16
    rows = total // BLOCKS
    packed[0, total:] = extra_low
    outs = []
    for e, which in enumerate((1 - core, core)):
        part = pl.ds(pl.multiple_of(which * (width // 2), 16), width // 2)
        for n in range(4):
            if n == 0:
                grad = dot(x_t[part, :here], query_t[...], 1, 1)
            elif n == 1:
                grad = dot(att_t[part, :], grad_attn[...])
            else:
                grad = dot(x_t[part, :], (grad_key, grad_value)[n - 2][...])
            store_blocks(packed, e, n, grad.astype(bf16), (flip_send, flip_keep)[e], rows)
        if e == 0:
            outs.append(fetch(packed.at[0], send_h, o_sems.at[0]))
        else:
            outs.append(fetch(packed.at[1, pl.ds(0, total)], keep_h, o_sems.at[1]))
    for copy in outs:
        copy.wait()


def tokens_kernel(grad_sum1, grad_query, grad_key, grad_value, wq, wk, wv, after, own, other):
    here = grad_sum1.shape[0]
    w_key, w_value = wk[...], wv[...]
    other[...] = (
        dot(grad_key[here:], w_key, 1, 1) + dot(grad_value[here:], w_value, 1, 1)
    ).astype(bf16)
    own[...] = (
        grad_sum1[...]
        + dot(grad_query[...], wq[...], 1, 1)
        + dot(grad_key[:here], w_key, 1, 1)
        + dot(grad_value[:here], w_value, 1, 1)
    )


def unpack_kernel(parts, held, scal, *refs):
    sources, refs = refs[: len(parts)], refs[len(parts) + held :]
    outs, (mark, scratch, sems) = refs[:6], refs[6:]
    mark[...] = jnp.zeros_like(mark)
    width = sources[0].shape[1]
    rows = sources[0].shape[0] // 4
    half = width // 2
    for slot, (source, (n, own, quarter)) in enumerate(zip(sources, parts)):
        which = scal[1] if own else 1 - scal[1]
        flip = scal[2 + 2 * n + (not own)]
        place = quarter ^ (flip // 4)
        for i in range(4):
            start = pl.multiple_of((i ^ (flip % 4)) * rows, 16)
            scratch[slot, i * rows : (i + 1) * rows, :] = source[pl.ds(start, rows), :].astype(f32)
        part, sem = scratch.at[slot], sems.at[slot]
        start = pl.multiple_of((which * 2 + place) * width, 128)
        if n == 0:
            fetch(part, outs[0].at[pl.ds(start, width), :], sem)
        elif n == 1:
            fetch(part, outs[1].at[:, pl.ds(start, width)], sem)
        else:
            target = pl.ds(pl.multiple_of(which * half, 16), half)
            for group in range(2):
                @pl.when(place == group)
                def _():
                    for i in range(2):
                        fetch(
                            scratch.at[slot, pl.ds(i * half, half)],
                            outs[2 + 2 * group + i].at[target, :],
                            sem,
                        )
    for slot in range(len(parts)):
        part = scratch.at[slot]
        pltpu.make_async_copy(part, part, sems.at[slot]).wait()


def call(kernel, in_specs, out_shapes, out_specs, scratch, vmem, moved=0, aliases=None):
    return pl.pallas_call(
        kernel,
        in_specs=in_specs,
        out_shape=out_shapes,
        out_specs=out_specs,
        scratch_shapes=scratch,
        input_output_aliases=aliases or {},
        compiler_params=pltpu.CompilerParams(vmem_limit_bytes=vmem * 2**20),
        cost_estimate=pl.CostEstimate(flops=0, bytes_accessed=moved, transcendentals=0),
    )


SEQ, CORE, NEAR, LINE, FAR = range(5)

STEPS = (
    ((NEAR, SEQ), (LINE, NEAR), (SEQ, LINE)),
    ((SEQ, LINE), (NEAR, SEQ), (LINE, NEAR)),
    ((LINE, NEAR), (SEQ, LINE), (NEAR, SEQ)),
)
BLOCKS = 8
UNPACK_VMEM = 56


def flip_of(index, pairs, core):
    bits = [(index >> pair[core]) & 1 for pair in pairs]
    return sum(b << (len(pairs) - 1 - n) for n, b in enumerate(bits))


def swap(values, pair, count):
    perm = [(i, i ^ (1 << pair[(i >> CORE) & 1])) for i in range(count)]
    return lax.ppermute(values, AXES, perm)


class Order:
    def __init__(self):
        self.passed = []

    def after(self, values, before):
        values, before = lax.optimization_barrier((values, before))
        self.passed += before
        return values


def halve(keep, got, extra, more_halves):
    size = keep.shape[0]
    if extra is not None:
        extra = extra + got[size:]
    if not more_halves:
        return keep + got[:size], None, extra
    half = size // 2
    send = keep[half:] + got[half:size]
    if extra is not None:
        send = jnp.concatenate([send, extra], 0)
    return keep[:half] + got[:half], send, extra


def sum_stream(order, keep, send, pairs, more, count, extra=None, before=None):
    steps = ((CORE, CORE),) + pairs
    for n, pair in enumerate(steps):
        got = swap(send, pair, count)
        if n == 2 and before is not None:
            keep, got = order.after((keep, got), [before])
        keep, send, extra = halve(keep, got, extra, n < len(steps) - 1)
    size = keep.shape[0]
    for pair in more:
        both = keep if extra is None else jnp.concatenate([keep, extra], 0)
        both = both + swap(both, pair, count)
        keep, extra = both[:size], None if extra is None else both[size:]
    for pair in reversed(pairs[1:]):
        keep = jnp.concatenate([keep, swap(keep, pair, count)], 0)
    return keep, swap(keep, pairs[0], count), swap(keep, (CORE, CORE), count), extra


def body(
    count, tokens, segment_ids, w_query, b_query, w_key, w_value, b_value, w_out, b_out,
    gain_attn, shift_attn, w_up, b_up, w_down, b_down, gain_ffn, shift_ffn, w_head, cot_out,
    cot_weight,
):
    row_count, here, width = tokens.shape
    hidden = w_up.shape[1]
    heads = width // HD
    keys = segment_ids.shape[1]
    bits = count.bit_length() - 1
    share = hidden // 2

    seq = lax.axis_index("seq")
    index = lax.axis_index("batch") * 2 + seq
    core = (index >> CORE) & 1
    more = [(b, b) for b in range(FAR, bits)]
    scal = [seq, core]
    for pairs in STEPS:
        flips = [flip_of(index, pairs, c) for c in (0, 1)]
        scal.append(jnp.where(core == 0, flips[0], flips[1]))
        scal.append(jnp.where(core == 0, flips[1], flips[0]))
    scal = jnp.stack([jnp.asarray(v, jnp.int32) for v in scal])

    x_own = tokens.reshape(here, width)
    x_oth = lax.ppermute(x_own, "seq", [(0, 1), (1, 0)])
    sds = jax.ShapeDtypeStruct
    dma = pltpu.SemaphoreType.DMA

    q, k_own, v_own = call(
        project_kernel,
        [VMEM] * 6,
        [sds((here, width), bf16)] * 3,
        [VMEM] * 3,
        [],
        56,
    )(x_own, w_query, b_query, w_key, w_value, b_value)

    square, up, down = (
        pltpu.VMEM(x, bf16) for x in ((width, width), (width, hidden), (hidden, width))
    )
    (
        layer_out, term, probs, k_all, v_all, att_t, grad_sum1, grad_attn, grad_mix, vecs,
        send_d, keep_d, send_u, keep_u,
    ) = call(
        middle_kernel,
        [SMEM] + [VMEM] * 17 + [HBM] * 5,
        [
            sds((here, width), bf16),
            sds((1, here), f32),
            sds((heads, keys, here), bf16),
            sds((keys, width), bf16),
            sds((keys, width), bf16),
            sds((width, here), bf16),
            sds((here, width), f32),
            sds((here, width), bf16),
            sds((here, width), bf16),
            sds((16, width), f32),
        ]
        + [sds((share, width), bf16)] * 4,
        [VMEM, VMEM, HBM] + [VMEM] * 7 + [HBM] * 4,
        [
            square,
            square,
            square,
            up,
            down,
            pltpu.VMEM((width, keys), bf16),
            pltpu.VMEM((heads, keys, here), bf16),
            pltpu.VMEM((here, hidden), bf16),
            pltpu.VMEM((here, hidden), bf16),
            pltpu.VMEM((2, share, width), bf16),
            pltpu.VMEM((2, share, width), bf16),
            dma((5,)),
            dma((heads // 2,)),
            dma((4,)),
        ],
        58,
    )(
        scal, x_own, x_oth, q, k_own, v_own, segment_ids, b_value, b_out, gain_attn, shift_attn,
        b_up, b_down, gain_ffn, shift_ffn, w_head, cot_out.reshape(here, width), cot_weight,
        w_key, w_value, w_out, w_up, w_down,
    )

    def unpack(parts, sources, held, after):
        targets = [(hidden, width), (width, hidden)] + [(width, width)] * 4
        *outs, mark = call(
            partial(unpack_kernel, parts, len(held) + len(after)),
            [SMEM] + [VMEM] * len(sources) + [HBM] * (len(held) + len(after)),
            [sds(x, f32) for x in targets] + [sds((8, 128), f32)],
            [pl.BlockSpec(memory_space=pltpu.HBM)] * 6 + [VMEM],
            [pltpu.VMEM((len(parts), width, width), f32), dma((len(parts),))],
            UNPACK_VMEM,
            0,
            {1 + len(sources) + i: i for i in range(len(held))},
        )(scal, *sources, *held, *after)
        return outs, mark

    grad_query, grad_key, grad_value, extra, send_q, keep_q = call(
        attention_back_kernel,
        [SMEM] + [VMEM] * 5 + [HBM] + [VMEM] * 4 + [HBM],
        [
            sds((here, width), bf16),
            sds((keys, width), bf16),
            sds((keys, width), bf16),
            sds((16, width), bf16),
            sds((share + 16, width), bf16),
            sds((share, width), bf16),
        ],
        [VMEM] * 4 + [HBM] * 2,
        [
            pltpu.VMEM((heads, keys, here), bf16),
            pltpu.VMEM((width, keys), bf16),
            pltpu.VMEM((width, keys), bf16),
            pltpu.VMEM((width, here), bf16),
            pltpu.VMEM((16, width), f32),
            pltpu.VMEM((2, share + 16, width), bf16),
            dma((heads // 2,)),
            dma((2,)),
        ],
        56,
    )(
        scal, x_own, x_oth, q, k_all, v_all, probs, att_t, grad_attn, grad_mix, vecs,
        send_u,
    )
    own, other = call(
        tokens_kernel,
        [VMEM] * 7 + [HBM],
        [sds((here, width), f32), sds((here, width), bf16)],
        [VMEM] * 2,
        [],
        16,
    )(grad_sum1, grad_query, grad_key, grad_value, w_query, w_key, w_value, extra)
    received = lax.ppermute(other, "seq", [(0, 1), (1, 0)])

    order = Order()
    sums = [
        sum_stream(order, keep_d, send_d, STEPS[0], more, count),
        sum_stream(order, keep_u, send_u, STEPS[1], more, count, None, other),
        sum_stream(order, keep_q, send_q, STEPS[2], more, count, extra),
    ]
    vec = sums[2][3].astype(f32)
    small = [vec[n] for n in range(13)] + [vec[4:8].reshape(-1)]
    small, own = lax.optimization_barrier((small, own))
    grad_tokens = own + received.astype(f32)

    early = [x for n in range(3) for x in (sums[n][0], sums[n][2])]
    parts = tuple((n, o, 0) for n in range(3) for o in (True, False))
    outs, mark = unpack(parts, early, [], [grad_tokens])
    gots = order.after([sums[n][1] for n in range(3)], [mark])
    others = [swap(got, (CORE, CORE), count) for got in gots]
    outs, mark = unpack(tuple((n, True, 1) for n in range(3)), gots, outs, [])
    outs, mark = unpack(
        tuple((n, False, 1) for n in range(3)), others, outs, order.passed + [mark]
    )
    grad_w_down, grad_w_up, grad_w_query, grad_w_out, grad_w_key, grad_w_value = outs
    return (
        layer_out.reshape(row_count, here, width),
        term.reshape(row_count, here),
        grad_tokens.reshape(row_count, here, width),
        grad_w_query,
        small[11],
        grad_w_key,
        grad_w_value,
        small[12],
        grad_w_out,
        small[10],
        small[8],
        small[9],
        grad_w_up,
        small[13],
        grad_w_down,
        small[3],
        small[1],
        small[2],
        small[0],
    )


def solution(mesh):
    rows, places = P("batch", "seq", None), P("batch", "seq")
    in_specs = (rows, P("batch", None)) + (P(),) * 16 + (rows, places)
    out_specs = (rows, places, rows) + (P(),) * 16
    count = mesh.shape["batch"] * mesh.shape["seq"]
    return jax.shard_map(
        partial(body, count), mesh=mesh, in_specs=in_specs, out_specs=out_specs, check_vma=False
    )
```

```python
from functools import partial

import jax
import jax.numpy as jnp
from jax import lax
from jax.experimental import pallas as pl
from jax.experimental.pallas import tpu as pltpu
from jax.sharding import PartitionSpec as P

HD = 64
EPS = 1e-06
MASKED = -1e30
bf16 = jnp.bfloat16
f32 = jnp.float32
AXES = ("batch", "seq")
PAIR = 2 * HD
VMEM = pl.BlockSpec(memory_space=pltpu.VMEM)
SMEM = pl.BlockSpec(memory_space=pltpu.SMEM)
HBM = pl.BlockSpec(memory_space=pl.ANY)


def dot(left, right, left_dim=1, right_dim=0):
    dims = (((left_dim,), (right_dim,)), ((), ()))
    return lax.dot_general(left, right, dims, preferred_element_type=f32)


def fetch(source, target, sem):
    copy = pltpu.make_async_copy(source, target, sem)
    copy.start()
    return copy


def column(row):
    return jnp.transpose(jnp.broadcast_to(row, (128, row.shape[1])))[:, :1]


def row_of(col):
    return jnp.transpose(jnp.broadcast_to(col, (col.shape[0], 128)))[:1]


def line(ref, part=slice(None)):
    return ref[part].reshape(1, -1)


def half_masks():
    lane = lax.broadcasted_iota(jnp.int32, (1, PAIR), 1)
    low = (lane < HD).astype(f32)
    return low.astype(bf16), (1.0 - low).astype(bf16)


def store_blocks(out, at, group, values, flip, rows):
    per = values.shape[0] // rows
    for i in range(per):
        place = (group * per + i) ^ flip
        start = pl.multiple_of(place * rows, 16)
        out[at, pl.ds(start, rows), :] = values[i * rows : (i + 1) * rows]


def project_kernel(x, wq, bq, wk, wv, bv, q, k, v):
    t = x[...]
    q[...] = (dot(t, wq[...]) + line(bq)).astype(bf16) * bf16(HD**-0.5)
    k[...] = dot(t, wk[...]).astype(bf16)
    v[...] = (dot(t, wv[...]) + line(bv)).astype(bf16)


def norm_forward(values):
    centered = values - jnp.mean(values, -1, keepdims=True)
    inverse = lax.rsqrt(jnp.mean(centered * centered, -1, keepdims=True) + EPS)
    return centered * inverse, inverse


def norm_backward(grad, gain, normed, inverse):
    g = grad * gain
    return inverse * (
        g - jnp.mean(g, -1, keepdims=True) - normed * jnp.mean(g * normed, -1, keepdims=True)
    )


def middle_kernel(
    scal, x_own, x_oth, q, k_own, v_own, seg, bv, b_out, gain1, shift1, b_up, b_down,
    gain2, shift2, w_head, cot, cot_weight, wk_h, wv_h, w_out_h, w_up_h, w_down_h,
    layer_out, term, probs_h, k_all, v_all, att_t, grad_sum1, grad_attn, grad_mix, vecs,
    send_d, keep_d, send_u, keep_u,
    wk, wv, w_out, w_up, w_down, v_t, probs, active, slope, packed_d, packed_u,
    w_sems, p_sems, o_sems,
):
    loads = [
        fetch(a, b, w_sems.at[n])
        for n, (a, b) in enumerate(
            ((wk_h, wk), (wv_h, wv), (w_out_h, w_out), (w_up_h, w_up), (w_down_h, w_down))
        )
    ]
    here, width = x_own.shape
    half, core = scal[0], scal[1]
    heads = width // HD
    loads[0].wait()
    loads[1].wait()
    other = x_oth[...]
    k_all[:here] = k_own[...]
    v_all[:here] = v_own[...]
    k_all[here:] = dot(other, wk[...]).astype(bf16)
    v_all[here:] = (dot(other, wv[...]) + line(bv)).astype(bf16)
    v_t[...] = jnp.transpose(v_all[...])

    own_ids = seg[:, pl.ds(pl.multiple_of(half * here, 128), here)].astype(f32)
    oth_ids = seg[:, pl.ds(pl.multiple_of((1 - half) * here, 128), here)].astype(f32)
    key_ids = jnp.concatenate([own_ids, oth_ids], 1)
    bias = jnp.where(column(key_ids) == own_ids, 0.0, MASKED)
    masks = half_masks()
    stores = []
    for p in range(heads // 2):
        lanes = slice(p * PAIR, (p + 1) * PAIR)
        q_pair, k_pair = q[:, lanes], k_all[:, lanes]
        for e in range(2):
            h = 2 * p + e
            scores = dot(k_pair, q_pair * masks[e], 1, 1) + bias
            weights = jnp.exp(scores - jnp.max(scores, 0, keepdims=True))
            weights = weights * (1.0 / jnp.sum(weights, 0, keepdims=True))
            low = weights.astype(bf16)
            probs[h] = low
            att_t[h * HD : (h + 1) * HD] = dot(v_t[h * HD : (h + 1) * HD], low).astype(bf16)
        stores.append(fetch(probs.at[pl.ds(2 * p, 2)], probs_h.at[pl.ds(2 * p, 2)], p_sems.at[p]))

    loads[2].wait()
    attn_out = dot(att_t[...], w_out[...], 0, 0) + line(b_out)
    n1, i1 = norm_forward(x_own[...].astype(f32) + attn_out)
    first = n1 * line(gain1) + line(shift1)
    f_low = first.astype(bf16)

    loads[3].wait()
    loads[4].wait()
    down = first + line(b_down)
    chunk = 512
    for j in range(w_up.shape[1] // chunk):
        cols = slice(j * chunk, (j + 1) * chunk)
        u = dot(f_low, w_up[:, cols]) + line(b_up, cols)
        cdf = 0.5 + 0.5 * lax.erf(u * (2.0**-0.5))
        pdf = jnp.exp(-0.5 * u * u) * 0.3989422804014327
        slope[:, cols] = (cdf + u * pdf).astype(bf16)
        act = (u * cdf).astype(bf16)
        active[:, cols] = act
        down = down + dot(act, w_down[cols, :])

    n2, i2 = norm_forward(down)
    second = n2 * line(gain2) + line(shift2)
    layer_out[...] = second.astype(bf16)
    head = line(w_head).astype(f32)
    logits = jnp.sum(second * head, -1, keepdims=True)
    softplus = jnp.maximum(logits, 0.0) + jnp.log1p(jnp.exp(-jnp.abs(logits)))
    term[...] = row_of(softplus)
    grad_logits = column(cot_weight[...]) * lax.logistic(logits)
    vecs[0:1] = jnp.sum(grad_logits * second, 0, keepdims=True)
    grad_second = cot[...].astype(f32) + grad_logits * head
    vecs[1:2] = jnp.sum(grad_second * n2, 0, keepdims=True)
    vecs[2:3] = jnp.sum(grad_second, 0, keepdims=True)
    g_sum2 = norm_backward(grad_second, line(gain2), n2, i2)
    g_down = g_sum2.astype(bf16)
    vecs[3:4] = jnp.sum(g_down.astype(f32), 0, keepdims=True)
    vecs[11:] = jnp.zeros((5, width), f32)

    rows = packed_d.shape[1] // BLOCKS
    outs = []
    halves = (1 - core, core)
    for e, which in enumerate(halves):
        for j in range(2):
            start = pl.multiple_of((which * 2 + j) * width, 128)
            grad = dot(active[:, pl.ds(start, width)], g_down, 0, 0).astype(bf16)
            store_blocks(packed_d, e, j, grad, scal[3 - e], rows)
        outs.append(fetch(packed_d.at[e], (send_d, keep_d)[e], o_sems.at[e]))

    first_t = jnp.transpose(f_low)
    grad_first = g_sum2
    for e, which in enumerate(halves):
        for j in range(2):
            start = pl.multiple_of((which * 2 + j) * width, 128)
            part = pl.ds(start, width)
            g_active = dot(g_down, w_down[part, :], 1, 1)
            g_upper = (g_active * slope[:, part].astype(f32)).astype(bf16)
            vecs[pl.ds(4 + which * 2 + j, 1), :] = jnp.sum(g_upper.astype(f32), 0, keepdims=True)
            grad = dot(first_t, g_upper).astype(bf16)
            store_blocks(packed_u, e, j, grad, scal[5 - e], rows)
            grad_first = grad_first + dot(g_upper, w_up[:, part], 1, 1)
        outs.append(fetch(packed_u.at[e], (send_u, keep_u)[e], o_sems.at[2 + e]))

    vecs[8:9] = jnp.sum(grad_first * n1, 0, keepdims=True)
    vecs[9:10] = jnp.sum(grad_first, 0, keepdims=True)
    g_sum1 = norm_backward(grad_first, line(gain1), n1, i1)
    grad_sum1[...] = g_sum1
    g_attn = g_sum1.astype(bf16)
    grad_attn[...] = g_attn
    vecs[10:11] = jnp.sum(g_attn.astype(f32), 0, keepdims=True)
    grad_mix[...] = dot(g_attn, w_out[...], 1, 1).astype(bf16)
    for copy in stores + outs:
        copy.wait()


def attention_back_kernel(
    scal, x_own, x_oth, q, k_all, v_all, probs_h, att_t, grad_attn, grad_mix, vecs, after,
    grad_query, grad_key, grad_value, extra, send_h, keep_h,
    probs, k_t, x_t, query_t, vec_all, packed, p_sems, o_sems,
):
    here = x_own.shape[0]
    core, flip_keep, flip_send = scal[1], scal[6], scal[7]
    width = q.shape[1]
    heads = width // HD
    loads = [
        fetch(probs_h.at[pl.ds(2 * p, 2)], probs.at[pl.ds(2 * p, 2)], p_sems.at[p])
        for p in range(heads // 2)
    ]
    k_t[...] = jnp.transpose(k_all[...])
    masks = half_masks()
    for p in range(heads // 2):
        lanes = slice(p * PAIR, (p + 1) * PAIR)
        mix_pair, q_pair, v_pair = grad_mix[:, lanes], q[:, lanes], v_all[:, lanes]
        mixes = [mix_pair * m for m in masks]
        queries = [q_pair * m for m in masks]
        loads[p].wait()
        grads = []
        for e in range(2):
            h = 2 * p + e
            weights = probs[h].astype(f32)
            product = weights * dot(v_pair, mixes[e], 1, 1)
            delta = jnp.sum(product, 0, keepdims=True)
            grad_scores = (product - weights * delta).astype(bf16)
            grads.append(grad_scores)
            query_t[h * HD : (h + 1) * HD] = (
                dot(k_t[h * HD : (h + 1) * HD], grad_scores) * (HD**-0.5)
            ).astype(bf16)
        both = jnp.concatenate([probs[2 * p], probs[2 * p + 1]], 1)
        grad_value[:, lanes] = dot(both, jnp.concatenate(mixes, 0)).astype(bf16)
        grad_key[:, lanes] = dot(
            jnp.concatenate(grads, 1), jnp.concatenate(queries, 0)
        ).astype(bf16)
    grad_query[...] = jnp.transpose(query_t[...])
    x_t[:, :here] = jnp.transpose(x_own[...])
    x_t[:, here:] = jnp.transpose(x_oth[...])

    vec_all[...] = vecs[...]
    vec_all[11:12] = jnp.sum(grad_query[...].astype(f32), 0, keepdims=True)
    vec_all[12:13] = jnp.sum(grad_value[...].astype(f32), 0, keepdims=True)
    extra_low = vec_all[...].astype(bf16)
    extra[...] = extra_low

    total = packed.shape[1] - 16
    rows = total // BLOCKS
    packed[0, total:] = extra_low
    outs = []
    for e, which in enumerate((1 - core, core)):
        part = pl.ds(pl.multiple_of(which * (width // 2), 16), width // 2)
        for n in range(4):
            if n == 0:
                grad = dot(x_t[part, :here], query_t[...], 1, 1)
            elif n == 1:
                grad = dot(att_t[part, :], grad_attn[...])
            else:
                grad = dot(x_t[part, :], (grad_key, grad_value)[n - 2][...])
            store_blocks(packed, e, n, grad.astype(bf16), (flip_send, flip_keep)[e], rows)
        if e == 0:
            outs.append(fetch(packed.at[0], send_h, o_sems.at[0]))
        else:
            outs.append(fetch(packed.at[1, pl.ds(0, total)], keep_h, o_sems.at[1]))
    for copy in outs:
        copy.wait()


def tokens_kernel(grad_sum1, grad_query, grad_key, grad_value, wq, wk, wv, after, own, other):
    here = grad_sum1.shape[0]
    w_key, w_value = wk[...], wv[...]
    other[...] = (
        dot(grad_key[here:], w_key, 1, 1) + dot(grad_value[here:], w_value, 1, 1)
    ).astype(bf16)
    own[...] = (
        grad_sum1[...]
        + dot(grad_query[...], wq[...], 1, 1)
        + dot(grad_key[:here], w_key, 1, 1)
        + dot(grad_value[:here], w_value, 1, 1)
    )


def unpack_kernel(parts, held, scal, *refs):
    sources, refs = refs[: len(parts)], refs[len(parts) + held :]
    outs, (mark, scratch, sems) = refs[:6], refs[6:]
    mark[...] = jnp.zeros_like(mark)
    width = sources[0].shape[1]
    rows = sources[0].shape[0] // 4
    half = width // 2
    for slot, (source, (n, own, quarter)) in enumerate(zip(sources, parts)):
        which = scal[1] if own else 1 - scal[1]
        flip = scal[2 + 2 * n + (not own)]
        place = quarter ^ (flip // 4)
        for i in range(4):
            start = pl.multiple_of((i ^ (flip % 4)) * rows, 16)
            scratch[slot, i * rows : (i + 1) * rows, :] = source[pl.ds(start, rows), :].astype(f32)
        part, sem = scratch.at[slot], sems.at[slot]
        start = pl.multiple_of((which * 2 + place) * width, 128)
        if n == 0:
            fetch(part, outs[0].at[pl.ds(start, width), :], sem)
        elif n == 1:
            fetch(part, outs[1].at[:, pl.ds(start, width)], sem)
        else:
            target = pl.ds(pl.multiple_of(which * half, 16), half)
            for group in range(2):
                @pl.when(place == group)
                def _():
                    for i in range(2):
                        fetch(
                            scratch.at[slot, pl.ds(i * half, half)],
                            outs[2 + 2 * group + i].at[target, :],
                            sem,
                        )
    for slot in range(len(parts)):
        part = scratch.at[slot]
        pltpu.make_async_copy(part, part, sems.at[slot]).wait()


def call(kernel, in_specs, out_shapes, out_specs, scratch, vmem, moved=0, aliases=None):
    return pl.pallas_call(
        kernel,
        in_specs=in_specs,
        out_shape=out_shapes,
        out_specs=out_specs,
        scratch_shapes=scratch,
        input_output_aliases=aliases or {},
        compiler_params=pltpu.CompilerParams(vmem_limit_bytes=vmem * 2**20),
        cost_estimate=pl.CostEstimate(flops=0, bytes_accessed=moved, transcendentals=0),
    )


SEQ, CORE, NEAR, LINE, FAR = range(5)

STEPS = (
    ((NEAR, SEQ), (LINE, NEAR), (SEQ, LINE)),
    ((SEQ, LINE), (NEAR, SEQ), (LINE, NEAR)),
    ((LINE, NEAR), (SEQ, LINE), (NEAR, SEQ)),
)
BLOCKS = 8
UNPACK_VMEM = 24


def flip_of(index, pairs, core):
    bits = [(index >> pair[core]) & 1 for pair in pairs]
    return sum(b << (len(pairs) - 1 - n) for n, b in enumerate(bits))


def swap(values, pair, count):
    perm = [(i, i ^ (1 << pair[(i >> CORE) & 1])) for i in range(count)]
    return lax.ppermute(values, AXES, perm)


class Order:
    def __init__(self):
        self.passed = []

    def after(self, values, before):
        values, before = lax.optimization_barrier((values, before))
        self.passed += before
        return values


def halve(keep, got, extra, more_halves):
    size = keep.shape[0]
    if extra is not None:
        extra = extra + got[size:]
    if not more_halves:
        return keep + got[:size], None, extra
    half = size // 2
    send = keep[half:] + got[half:size]
    if extra is not None:
        send = jnp.concatenate([send, extra], 0)
    return keep[:half] + got[:half], send, extra


def sum_stream(order, keep, send, pairs, more, count, extra=None, before=None, late=None):
    steps = ((CORE, CORE),) + pairs
    for n, pair in enumerate(steps):
        got = swap(send, pair, count)
        if n == 2 and before is not None:
            keep, got = order.after((keep, got), [before])
        keep, send, extra = halve(keep, got, extra, n < len(steps) - 1)
    size = keep.shape[0]
    for pair in more:
        both = keep if extra is None else jnp.concatenate([keep, extra], 0)
        both = both + swap(both, pair, count)
        keep, extra = both[:size], None if extra is None else both[size:]
    for n, pair in enumerate(reversed(pairs[1:])):
        got = swap(keep, pair, count)
        if n == 0 and late is not None:
            keep, got = order.after((keep, got), [late])
        keep = jnp.concatenate([keep, got], 0)
    return keep, swap(keep, pairs[0], count), swap(keep, (CORE, CORE), count), extra


def body(
    count, tokens, segment_ids, w_query, b_query, w_key, w_value, b_value, w_out, b_out,
    gain_attn, shift_attn, w_up, b_up, w_down, b_down, gain_ffn, shift_ffn, w_head, cot_out,
    cot_weight,
):
    row_count, here, width = tokens.shape
    hidden = w_up.shape[1]
    heads = width // HD
    keys = segment_ids.shape[1]
    bits = count.bit_length() - 1
    share = hidden // 2

    seq = lax.axis_index("seq")
    index = lax.axis_index("batch") * 2 + seq
    core = (index >> CORE) & 1
    more = [(b, b) for b in range(FAR, bits)]
    scal = [seq, core]
    for pairs in STEPS:
        flips = [flip_of(index, pairs, c) for c in (0, 1)]
        scal.append(jnp.where(core == 0, flips[0], flips[1]))
        scal.append(jnp.where(core == 0, flips[1], flips[0]))
    scal = jnp.stack([jnp.asarray(v, jnp.int32) for v in scal])

    x_own = tokens.reshape(here, width)
    x_oth = lax.ppermute(x_own, "seq", [(0, 1), (1, 0)])
    sds = jax.ShapeDtypeStruct
    dma = pltpu.SemaphoreType.DMA

    q, k_own, v_own = call(
        project_kernel,
        [VMEM] * 6,
        [sds((here, width), bf16)] * 3,
        [VMEM] * 3,
        [],
        56,
    )(x_own, w_query, b_query, w_key, w_value, b_value)

    square, up, down = (
        pltpu.VMEM(x, bf16) for x in ((width, width), (width, hidden), (hidden, width))
    )
    (
        layer_out, term, probs, k_all, v_all, att_t, grad_sum1, grad_attn, grad_mix, vecs,
        send_d, keep_d, send_u, keep_u,
    ) = call(
        middle_kernel,
        [SMEM] + [VMEM] * 17 + [HBM] * 5,
        [
            sds((here, width), bf16),
            sds((1, here), f32),
            sds((heads, keys, here), bf16),
            sds((keys, width), bf16),
            sds((keys, width), bf16),
            sds((width, here), bf16),
            sds((here, width), f32),
            sds((here, width), bf16),
            sds((here, width), bf16),
            sds((16, width), f32),
        ]
        + [sds((share, width), bf16)] * 4,
        [VMEM, VMEM, HBM] + [VMEM] * 7 + [HBM] * 4,
        [
            square,
            square,
            square,
            up,
            down,
            pltpu.VMEM((width, keys), bf16),
            pltpu.VMEM((heads, keys, here), bf16),
            pltpu.VMEM((here, hidden), bf16),
            pltpu.VMEM((here, hidden), bf16),
            pltpu.VMEM((2, share, width), bf16),
            pltpu.VMEM((2, share, width), bf16),
            dma((5,)),
            dma((heads // 2,)),
            dma((4,)),
        ],
        58,
    )(
        scal, x_own, x_oth, q, k_own, v_own, segment_ids, b_value, b_out, gain_attn, shift_attn,
        b_up, b_down, gain_ffn, shift_ffn, w_head, cot_out.reshape(here, width), cot_weight,
        w_key, w_value, w_out, w_up, w_down,
    )

    def unpack(parts, sources, held, after):
        targets = [(hidden, width), (width, hidden)] + [(width, width)] * 4
        *outs, mark = call(
            partial(unpack_kernel, parts, len(held) + len(after)),
            [SMEM] + [VMEM] * len(sources) + [HBM] * (len(held) + len(after)),
            [sds(x, f32) for x in targets] + [sds((8, 128), f32)],
            [pl.BlockSpec(memory_space=pltpu.HBM)] * 6 + [VMEM],
            [pltpu.VMEM((len(parts), width, width), f32), dma((len(parts),))],
            UNPACK_VMEM,
            0,
            {1 + len(sources) + i: i for i in range(len(held))},
        )(scal, *sources, *held, *after)
        return outs, mark

    grad_query, grad_key, grad_value, extra, send_q, keep_q = call(
        attention_back_kernel,
        [SMEM] + [VMEM] * 5 + [HBM] + [VMEM] * 4 + [HBM],
        [
            sds((here, width), bf16),
            sds((keys, width), bf16),
            sds((keys, width), bf16),
            sds((16, width), bf16),
            sds((share + 16, width), bf16),
            sds((share, width), bf16),
        ],
        [VMEM] * 4 + [HBM] * 2,
        [
            pltpu.VMEM((heads, keys, here), bf16),
            pltpu.VMEM((width, keys), bf16),
            pltpu.VMEM((width, keys), bf16),
            pltpu.VMEM((width, here), bf16),
            pltpu.VMEM((16, width), f32),
            pltpu.VMEM((2, share + 16, width), bf16),
            dma((heads // 2,)),
            dma((2,)),
        ],
        56,
    )(
        scal, x_own, x_oth, q, k_all, v_all, probs, att_t, grad_attn, grad_mix, vecs,
        send_u,
    )
    own, other = call(
        tokens_kernel,
        [VMEM] * 7 + [HBM],
        [sds((here, width), f32), sds((here, width), bf16)],
        [VMEM] * 2,
        [],
        16,
    )(grad_sum1, grad_query, grad_key, grad_value, w_query, w_key, w_value, extra)
    received = lax.ppermute(other, "seq", [(0, 1), (1, 0)])

    grad_tokens = own + received.astype(f32)

    order = Order()
    sums = [
        sum_stream(order, keep_d, send_d, STEPS[0], more, count, None, None, grad_tokens),
        sum_stream(order, keep_u, send_u, STEPS[1], more, count, None, other),
        sum_stream(order, keep_q, send_q, STEPS[2], more, count, extra),
    ]
    vec = sums[2][3].astype(f32)
    small = [vec[n] for n in range(13)] + [vec[4:8].reshape(-1)]
    early = [x for n in range(3) for x in (sums[n][0], sums[n][2])]
    small, early = lax.optimization_barrier((small, early))
    parts = tuple((n, o, 0) for n in range(3) for o in (True, False))
    outs, mark = unpack(parts, early, [], [])
    gots = order.after([sums[n][1] for n in range(3)], [mark])
    others = [swap(got, (CORE, CORE), count) for got in gots]
    outs, mark = unpack(tuple((n, True, 1) for n in range(3)), gots, outs, [])
    outs, mark = unpack(
        tuple((n, False, 1) for n in range(3)), others, outs, order.passed + [mark]
    )
    grad_w_down, grad_w_up, grad_w_query, grad_w_out, grad_w_key, grad_w_value = outs
    return (
        layer_out.reshape(row_count, here, width),
        term.reshape(row_count, here),
        grad_tokens.reshape(row_count, here, width),
        grad_w_query,
        small[11],
        grad_w_key,
        grad_w_value,
        small[12],
        grad_w_out,
        small[10],
        small[8],
        small[9],
        grad_w_up,
        small[13],
        grad_w_down,
        small[3],
        small[1],
        small[2],
        small[0],
    )


def solution(mesh):
    rows, places = P("batch", "seq", None), P("batch", "seq")
    in_specs = (rows, P("batch", None)) + (P(),) * 16 + (rows, places)
    out_specs = (rows, places, rows) + (P(),) * 16
    count = mesh.shape["batch"] * mesh.shape["seq"]
    return jax.shard_map(
        partial(body, count), mesh=mesh, in_specs=in_specs, out_specs=out_specs, check_vma=False
    )
```

```python
from functools import partial

import jax
import jax.numpy as jnp
from jax import lax
from jax.experimental import pallas as pl
from jax.experimental.pallas import tpu as pltpu
from jax.sharding import PartitionSpec as P

HD = 64
EPS = 1e-06
MASKED = -1e30
bf16 = jnp.bfloat16
f32 = jnp.float32
AXES = ("batch", "seq")
PAIR = 2 * HD
VMEM = pl.BlockSpec(memory_space=pltpu.VMEM)
SMEM = pl.BlockSpec(memory_space=pltpu.SMEM)
HBM = pl.BlockSpec(memory_space=pl.ANY)


def dot(left, right, left_dim=1, right_dim=0):
    dims = (((left_dim,), (right_dim,)), ((), ()))
    return lax.dot_general(left, right, dims, preferred_element_type=f32)


def fetch(source, target, sem):
    copy = pltpu.make_async_copy(source, target, sem)
    copy.start()
    return copy


def column(row):
    return jnp.transpose(jnp.broadcast_to(row, (128, row.shape[1])))[:, :1]


def row_of(col):
    return jnp.transpose(jnp.broadcast_to(col, (col.shape[0], 128)))[:1]


def line(ref, part=slice(None)):
    return ref[part].reshape(1, -1)


def half_masks():
    lane = lax.broadcasted_iota(jnp.int32, (1, PAIR), 1)
    low = (lane < HD).astype(f32)
    return low.astype(bf16), (1.0 - low).astype(bf16)


def store_blocks(out, at, group, values, flip, rows):
    per = values.shape[0] // rows
    for i in range(per):
        place = (group * per + i) ^ flip
        start = pl.multiple_of(place * rows, 16)
        out[at, pl.ds(start, rows), :] = values[i * rows : (i + 1) * rows]


def project_kernel(x, wq, bq, wk, wv, bv, q, k, v):
    t = x[...]
    q[...] = (dot(t, wq[...]) + line(bq)).astype(bf16) * bf16(HD**-0.5)
    k[...] = dot(t, wk[...]).astype(bf16)
    v[...] = (dot(t, wv[...]) + line(bv)).astype(bf16)


def norm_forward(values):
    centered = values - jnp.mean(values, -1, keepdims=True)
    inverse = lax.rsqrt(jnp.mean(centered * centered, -1, keepdims=True) + EPS)
    return centered * inverse, inverse


def norm_backward(grad, gain, normed, inverse):
    g = grad * gain
    return inverse * (
        g - jnp.mean(g, -1, keepdims=True) - normed * jnp.mean(g * normed, -1, keepdims=True)
    )


def middle_kernel(
    scal, x_own, x_oth, q, k_own, v_own, seg, bv, b_out, gain1, shift1, b_up, b_down,
    gain2, shift2, w_head, cot, cot_weight, wk_h, wv_h, w_out_h, w_up_h, w_down_h,
    layer_out, term, probs_h, k_all, v_all, att_t, grad_sum1, grad_attn, grad_mix, vecs,
    send_d, keep_d, send_u, keep_u,
    wk, wv, w_out, w_up, w_down, v_t, probs, active, slope, packed_d, packed_u,
    w_sems, p_sems, o_sems,
):
    loads = [
        fetch(a, b, w_sems.at[n])
        for n, (a, b) in enumerate(
            ((wk_h, wk), (wv_h, wv), (w_out_h, w_out), (w_up_h, w_up), (w_down_h, w_down))
        )
    ]
    here, width = x_own.shape
    half, core = scal[0], scal[1]
    heads = width // HD
    loads[0].wait()
    loads[1].wait()
    other = x_oth[...]
    k_all[:here] = k_own[...]
    v_all[:here] = v_own[...]
    k_all[here:] = dot(other, wk[...]).astype(bf16)
    v_all[here:] = (dot(other, wv[...]) + line(bv)).astype(bf16)
    v_t[...] = jnp.transpose(v_all[...])

    own_ids = seg[:, pl.ds(pl.multiple_of(half * here, 128), here)].astype(f32)
    oth_ids = seg[:, pl.ds(pl.multiple_of((1 - half) * here, 128), here)].astype(f32)
    key_ids = jnp.concatenate([own_ids, oth_ids], 1)
    bias = jnp.where(column(key_ids) == own_ids, 0.0, MASKED)
    masks = half_masks()
    stores = []
    for p in range(heads // 2):
        lanes = slice(p * PAIR, (p + 1) * PAIR)
        q_pair, k_pair = q[:, lanes], k_all[:, lanes]
        for e in range(2):
            h = 2 * p + e
            scores = dot(k_pair, q_pair * masks[e], 1, 1) + bias
            weights = jnp.exp(scores - jnp.max(scores, 0, keepdims=True))
            weights = weights * (1.0 / jnp.sum(weights, 0, keepdims=True))
            low = weights.astype(bf16)
            probs[h] = low
            att_t[h * HD : (h + 1) * HD] = dot(v_t[h * HD : (h + 1) * HD], low).astype(bf16)
        stores.append(fetch(probs.at[pl.ds(2 * p, 2)], probs_h.at[pl.ds(2 * p, 2)], p_sems.at[p]))

    loads[2].wait()
    attn_out = dot(att_t[...], w_out[...], 0, 0) + line(b_out)
    n1, i1 = norm_forward(x_own[...].astype(f32) + attn_out)
    first = n1 * line(gain1) + line(shift1)
    f_low = first.astype(bf16)

    loads[3].wait()
    loads[4].wait()
    down = first + line(b_down)
    chunk = 1024
    for j in range(w_up.shape[1] // chunk):
        cols = slice(j * chunk, (j + 1) * chunk)
        u = dot(f_low, w_up[:, cols]) + line(b_up, cols)
        cdf = 0.5 + 0.5 * lax.erf(u * (2.0**-0.5))
        pdf = jnp.exp(-0.5 * u * u) * 0.3989422804014327
        slope[:, cols] = (cdf + u * pdf).astype(bf16)
        act = (u * cdf).astype(bf16)
        active[:, cols] = act
        down = down + dot(act, w_down[cols, :])

    n2, i2 = norm_forward(down)
    second = n2 * line(gain2) + line(shift2)
    layer_out[...] = second.astype(bf16)
    head = line(w_head).astype(f32)
    logits = jnp.sum(second * head, -1, keepdims=True)
    softplus = jnp.maximum(logits, 0.0) + jnp.log1p(jnp.exp(-jnp.abs(logits)))
    term[...] = row_of(softplus)
    grad_logits = column(cot_weight[...]) * lax.logistic(logits)
    vecs[0:1] = jnp.sum(grad_logits * second, 0, keepdims=True)
    grad_second = cot[...].astype(f32) + grad_logits * head
    vecs[1:2] = jnp.sum(grad_second * n2, 0, keepdims=True)
    vecs[2:3] = jnp.sum(grad_second, 0, keepdims=True)
    g_sum2 = norm_backward(grad_second, line(gain2), n2, i2)
    g_down = g_sum2.astype(bf16)
    vecs[3:4] = jnp.sum(g_down.astype(f32), 0, keepdims=True)
    vecs[11:] = jnp.zeros((5, width), f32)

    rows = packed_d.shape[1] // BLOCKS
    outs = []
    halves = (1 - core, core)
    for e, which in enumerate(halves):
        for j in range(2):
            start = pl.multiple_of((which * 2 + j) * width, 128)
            grad = dot(active[:, pl.ds(start, width)], g_down, 0, 0).astype(bf16)
            store_blocks(packed_d, e, j, grad, scal[3 - e], rows)
        outs.append(fetch(packed_d.at[e], (send_d, keep_d)[e], o_sems.at[e]))

    first_t = jnp.transpose(f_low)
    grad_first = g_sum2
    for e, which in enumerate(halves):
        for j in range(2):
            start = pl.multiple_of((which * 2 + j) * width, 128)
            part = pl.ds(start, width)
            g_active = dot(g_down, w_down[part, :], 1, 1)
            g_upper = (g_active * slope[:, part].astype(f32)).astype(bf16)
            vecs[pl.ds(4 + which * 2 + j, 1), :] = jnp.sum(g_upper.astype(f32), 0, keepdims=True)
            grad = dot(first_t, g_upper).astype(bf16)
            store_blocks(packed_u, e, j, grad, scal[5 - e], rows)
            grad_first = grad_first + dot(g_upper, w_up[:, part], 1, 1)
        outs.append(fetch(packed_u.at[e], (send_u, keep_u)[e], o_sems.at[2 + e]))

    vecs[8:9] = jnp.sum(grad_first * n1, 0, keepdims=True)
    vecs[9:10] = jnp.sum(grad_first, 0, keepdims=True)
    g_sum1 = norm_backward(grad_first, line(gain1), n1, i1)
    grad_sum1[...] = g_sum1
    g_attn = g_sum1.astype(bf16)
    grad_attn[...] = g_attn
    vecs[10:11] = jnp.sum(g_attn.astype(f32), 0, keepdims=True)
    grad_mix[...] = dot(g_attn, w_out[...], 1, 1).astype(bf16)
    for copy in stores + outs:
        copy.wait()


def attention_back_kernel(
    scal, x_own, x_oth, q, k_all, v_all, probs_h, att_t, grad_attn, grad_mix, vecs, after,
    grad_query, grad_key, grad_value, extra, send_h, keep_h,
    probs, k_t, x_t, query_t, vec_all, packed, p_sems, o_sems,
):
    here = x_own.shape[0]
    core, flip_keep, flip_send = scal[1], scal[6], scal[7]
    width = q.shape[1]
    heads = width // HD
    loads = [
        fetch(probs_h.at[pl.ds(2 * p, 2)], probs.at[pl.ds(2 * p, 2)], p_sems.at[p])
        for p in range(heads // 2)
    ]
    k_t[...] = jnp.transpose(k_all[...])
    masks = half_masks()
    for p in range(heads // 2):
        lanes = slice(p * PAIR, (p + 1) * PAIR)
        mix_pair, q_pair, v_pair = grad_mix[:, lanes], q[:, lanes], v_all[:, lanes]
        mixes = [mix_pair * m for m in masks]
        queries = [q_pair * m for m in masks]
        loads[p].wait()
        grads = []
        for e in range(2):
            h = 2 * p + e
            weights = probs[h].astype(f32)
            product = weights * dot(v_pair, mixes[e], 1, 1)
            delta = jnp.sum(product, 0, keepdims=True)
            grad_scores = (product - weights * delta).astype(bf16)
            grads.append(grad_scores)
            query_t[h * HD : (h + 1) * HD] = (
                dot(k_t[h * HD : (h + 1) * HD], grad_scores) * (HD**-0.5)
            ).astype(bf16)
        both = jnp.concatenate([probs[2 * p], probs[2 * p + 1]], 1)
        grad_value[:, lanes] = dot(both, jnp.concatenate(mixes, 0)).astype(bf16)
        grad_key[:, lanes] = dot(
            jnp.concatenate(grads, 1), jnp.concatenate(queries, 0)
        ).astype(bf16)
    grad_query[...] = jnp.transpose(query_t[...])
    x_t[:, :here] = jnp.transpose(x_own[...])
    x_t[:, here:] = jnp.transpose(x_oth[...])

    vec_all[...] = vecs[...]
    vec_all[11:12] = jnp.sum(grad_query[...].astype(f32), 0, keepdims=True)
    vec_all[12:13] = jnp.sum(grad_value[...].astype(f32), 0, keepdims=True)
    extra_low = vec_all[...].astype(bf16)
    extra[...] = extra_low

    total = packed.shape[1] - 16
    rows = total // BLOCKS
    packed[0, total:] = extra_low
    outs = []
    for e, which in enumerate((1 - core, core)):
        part = pl.ds(pl.multiple_of(which * (width // 2), 16), width // 2)
        for n in range(4):
            if n == 0:
                grad = dot(x_t[part, :here], query_t[...], 1, 1)
            elif n == 1:
                grad = dot(att_t[part, :], grad_attn[...])
            else:
                grad = dot(x_t[part, :], (grad_key, grad_value)[n - 2][...])
            store_blocks(packed, e, n, grad.astype(bf16), (flip_send, flip_keep)[e], rows)
        if e == 0:
            outs.append(fetch(packed.at[0], send_h, o_sems.at[0]))
        else:
            outs.append(fetch(packed.at[1, pl.ds(0, total)], keep_h, o_sems.at[1]))
    for copy in outs:
        copy.wait()


def tokens_kernel(grad_sum1, grad_query, grad_key, grad_value, wq, wk, wv, after, own, other):
    here = grad_sum1.shape[0]
    w_key, w_value = wk[...], wv[...]
    other[...] = (
        dot(grad_key[here:], w_key, 1, 1) + dot(grad_value[here:], w_value, 1, 1)
    ).astype(bf16)
    own[...] = (
        grad_sum1[...]
        + dot(grad_query[...], wq[...], 1, 1)
        + dot(grad_key[:here], w_key, 1, 1)
        + dot(grad_value[:here], w_value, 1, 1)
    )


def unpack_kernel(parts, held, scal, *refs):
    sources, refs = refs[: len(parts)], refs[len(parts) + held :]
    outs, (mark, scratch, sems) = refs[:6], refs[6:]
    mark[...] = jnp.zeros_like(mark)
    width = sources[0].shape[1]
    rows = sources[0].shape[0] // 4
    half = width // 2
    for slot, (source, (n, own, quarter)) in enumerate(zip(sources, parts)):
        which = scal[1] if own else 1 - scal[1]
        flip = scal[2 + 2 * n + (not own)]
        place = quarter ^ (flip // 4)
        for i in range(4):
            start = pl.multiple_of((i ^ (flip % 4)) * rows, 16)
            scratch[slot, i * rows : (i + 1) * rows, :] = source[pl.ds(start, rows), :].astype(f32)
        part, sem = scratch.at[slot], sems.at[slot]
        start = pl.multiple_of((which * 2 + place) * width, 128)
        if n == 0:
            fetch(part, outs[0].at[pl.ds(start, width), :], sem)
        elif n == 1:
            fetch(part, outs[1].at[:, pl.ds(start, width)], sem)
        else:
            target = pl.ds(pl.multiple_of(which * half, 16), half)
            for group in range(2):
                @pl.when(place == group)
                def _():
                    for i in range(2):
                        fetch(
                            scratch.at[slot, pl.ds(i * half, half)],
                            outs[2 + 2 * group + i].at[target, :],
                            sem,
                        )
    for slot in range(len(parts)):
        part = scratch.at[slot]
        pltpu.make_async_copy(part, part, sems.at[slot]).wait()


def call(kernel, in_specs, out_shapes, out_specs, scratch, vmem, moved=0, aliases=None):
    return pl.pallas_call(
        kernel,
        in_specs=in_specs,
        out_shape=out_shapes,
        out_specs=out_specs,
        scratch_shapes=scratch,
        input_output_aliases=aliases or {},
        compiler_params=pltpu.CompilerParams(vmem_limit_bytes=vmem * 2**20),
        cost_estimate=pl.CostEstimate(flops=0, bytes_accessed=moved, transcendentals=0),
    )


SEQ, CORE, NEAR, LINE, FAR = range(5)

STEPS = (
    ((SEQ, LINE), (NEAR, SEQ), (LINE, NEAR)),
    ((LINE, NEAR), (SEQ, LINE), (NEAR, SEQ)),
    ((NEAR, SEQ), (LINE, NEAR), (SEQ, LINE)),
)
BLOCKS = 8
UNPACK_VMEM = 24


def flip_of(index, pairs, core):
    bits = [(index >> pair[core]) & 1 for pair in pairs]
    return sum(b << (len(pairs) - 1 - n) for n, b in enumerate(bits))


def swap(values, pair, count):
    perm = [(i, i ^ (1 << pair[(i >> CORE) & 1])) for i in range(count)]
    return lax.ppermute(values, AXES, perm)


class Order:
    def __init__(self):
        self.passed = []

    def after(self, values, before):
        values, before = lax.optimization_barrier((values, before))
        self.passed += before
        return values


def halve(keep, got, extra, more_halves):
    size = keep.shape[0]
    if extra is not None:
        extra = extra + got[size:]
    if not more_halves:
        return keep + got[:size], None, extra
    half = size // 2
    send = keep[half:] + got[half:size]
    if extra is not None:
        send = jnp.concatenate([send, extra], 0)
    return keep[:half] + got[:half], send, extra


def sum_stream(order, keep, send, pairs, more, count, extra=None, before=None, late=None):
    steps = ((CORE, CORE),) + pairs
    for n, pair in enumerate(steps):
        got = swap(send, pair, count)
        if n == 2 and before is not None:
            keep, got = order.after((keep, got), [before])
        keep, send, extra = halve(keep, got, extra, n < len(steps) - 1)
    size = keep.shape[0]
    for pair in more:
        both = keep if extra is None else jnp.concatenate([keep, extra], 0)
        both = both + swap(both, pair, count)
        keep, extra = both[:size], None if extra is None else both[size:]
    for n, pair in enumerate(reversed(pairs[1:])):
        got = swap(keep, pair, count)
        if n == 0 and late is not None:
            keep, got = order.after((keep, got), [late])
        keep = jnp.concatenate([keep, got], 0)
    return keep, swap(keep, pairs[0], count), swap(keep, (CORE, CORE), count), extra


def body(
    count, tokens, segment_ids, w_query, b_query, w_key, w_value, b_value, w_out, b_out,
    gain_attn, shift_attn, w_up, b_up, w_down, b_down, gain_ffn, shift_ffn, w_head, cot_out,
    cot_weight,
):
    row_count, here, width = tokens.shape
    hidden = w_up.shape[1]
    heads = width // HD
    keys = segment_ids.shape[1]
    bits = count.bit_length() - 1
    share = hidden // 2

    seq = lax.axis_index("seq")
    index = lax.axis_index("batch") * 2 + seq
    core = (index >> CORE) & 1
    more = [(b, b) for b in range(FAR, bits)]
    scal = [seq, core]
    for pairs in STEPS:
        flips = [flip_of(index, pairs, c) for c in (0, 1)]
        scal.append(jnp.where(core == 0, flips[0], flips[1]))
        scal.append(jnp.where(core == 0, flips[1], flips[0]))
    scal = jnp.stack([jnp.asarray(v, jnp.int32) for v in scal])

    x_own = tokens.reshape(here, width)
    x_oth = lax.ppermute(x_own, "seq", [(0, 1), (1, 0)])
    sds = jax.ShapeDtypeStruct
    dma = pltpu.SemaphoreType.DMA

    q, k_own, v_own = call(
        project_kernel,
        [VMEM] * 6,
        [sds((here, width), bf16)] * 3,
        [VMEM] * 3,
        [],
        56,
    )(x_own, w_query, b_query, w_key, w_value, b_value)

    square, up, down = (
        pltpu.VMEM(x, bf16) for x in ((width, width), (width, hidden), (hidden, width))
    )
    (
        layer_out, term, probs, k_all, v_all, att_t, grad_sum1, grad_attn, grad_mix, vecs,
        send_d, keep_d, send_u, keep_u,
    ) = call(
        middle_kernel,
        [SMEM] + [VMEM] * 17 + [HBM] * 5,
        [
            sds((here, width), bf16),
            sds((1, here), f32),
            sds((heads, keys, here), bf16),
            sds((keys, width), bf16),
            sds((keys, width), bf16),
            sds((width, here), bf16),
            sds((here, width), f32),
            sds((here, width), bf16),
            sds((here, width), bf16),
            sds((16, width), f32),
        ]
        + [sds((share, width), bf16)] * 4,
        [VMEM, VMEM, HBM] + [VMEM] * 7 + [HBM] * 4,
        [
            square,
            square,
            square,
            up,
            down,
            pltpu.VMEM((width, keys), bf16),
            pltpu.VMEM((heads, keys, here), bf16),
            pltpu.VMEM((here, hidden), bf16),
            pltpu.VMEM((here, hidden), bf16),
            pltpu.VMEM((2, share, width), bf16),
            pltpu.VMEM((2, share, width), bf16),
            dma((5,)),
            dma((heads // 2,)),
            dma((4,)),
        ],
        58,
    )(
        scal, x_own, x_oth, q, k_own, v_own, segment_ids, b_value, b_out, gain_attn, shift_attn,
        b_up, b_down, gain_ffn, shift_ffn, w_head, cot_out.reshape(here, width), cot_weight,
        w_key, w_value, w_out, w_up, w_down,
    )

    def unpack(parts, sources, held, after):
        targets = [(hidden, width), (width, hidden)] + [(width, width)] * 4
        *outs, mark = call(
            partial(unpack_kernel, parts, len(held) + len(after)),
            [SMEM] + [VMEM] * len(sources) + [HBM] * (len(held) + len(after)),
            [sds(x, f32) for x in targets] + [sds((8, 128), f32)],
            [pl.BlockSpec(memory_space=pltpu.HBM)] * 6 + [VMEM],
            [pltpu.VMEM((len(parts), width, width), f32), dma((len(parts),))],
            UNPACK_VMEM,
            0,
            {1 + len(sources) + i: i for i in range(len(held))},
        )(scal, *sources, *held, *after)
        return outs, mark

    grad_query, grad_key, grad_value, extra, send_q, keep_q = call(
        attention_back_kernel,
        [SMEM] + [VMEM] * 5 + [HBM] + [VMEM] * 4 + [HBM],
        [
            sds((here, width), bf16),
            sds((keys, width), bf16),
            sds((keys, width), bf16),
            sds((16, width), bf16),
            sds((share + 16, width), bf16),
            sds((share, width), bf16),
        ],
        [VMEM] * 4 + [HBM] * 2,
        [
            pltpu.VMEM((heads, keys, here), bf16),
            pltpu.VMEM((width, keys), bf16),
            pltpu.VMEM((width, keys), bf16),
            pltpu.VMEM((width, here), bf16),
            pltpu.VMEM((16, width), f32),
            pltpu.VMEM((2, share + 16, width), bf16),
            dma((heads // 2,)),
            dma((2,)),
        ],
        56,
    )(
        scal, x_own, x_oth, q, k_all, v_all, probs, att_t, grad_attn, grad_mix, vecs,
        send_u,
    )
    own, other = call(
        tokens_kernel,
        [VMEM] * 7 + [HBM],
        [sds((here, width), f32), sds((here, width), bf16)],
        [VMEM] * 2,
        [],
        16,
    )(grad_sum1, grad_query, grad_key, grad_value, w_query, w_key, w_value, extra)
    received = lax.ppermute(other, "seq", [(0, 1), (1, 0)])

    grad_tokens = own + received.astype(f32)

    order = Order()
    sums = [
        sum_stream(order, keep_d, send_d, STEPS[0], more, count, None, None, grad_tokens),
        sum_stream(order, keep_u, send_u, STEPS[1], more, count, None, other),
        sum_stream(order, keep_q, send_q, STEPS[2], more, count, extra),
    ]
    vec = sums[2][3].astype(f32)
    small = [vec[n] for n in range(13)] + [vec[4:8].reshape(-1)]
    early = [x for n in range(3) for x in (sums[n][0], sums[n][2])]
    small, early = lax.optimization_barrier((small, early))
    parts = tuple((n, o, 0) for n in range(3) for o in (True, False))
    outs, mark = unpack(parts, early, [], [])
    gots = order.after([sums[n][1] for n in range(3)], [mark])
    others = [swap(got, (CORE, CORE), count) for got in gots]
    outs, mark = unpack(tuple((n, True, 1) for n in range(3)), gots, outs, [])
    outs, mark = unpack(
        tuple((n, False, 1) for n in range(3)), others, outs, order.passed + [mark]
    )
    grad_w_down, grad_w_up, grad_w_query, grad_w_out, grad_w_key, grad_w_value = outs
    return (
        layer_out.reshape(row_count, here, width),
        term.reshape(row_count, here),
        grad_tokens.reshape(row_count, here, width),
        grad_w_query,
        small[11],
        grad_w_key,
        grad_w_value,
        small[12],
        grad_w_out,
        small[10],
        small[8],
        small[9],
        grad_w_up,
        small[13],
        grad_w_down,
        small[3],
        small[1],
        small[2],
        small[0],
    )


def solution(mesh):
    rows, places = P("batch", "seq", None), P("batch", "seq")
    in_specs = (rows, P("batch", None)) + (P(),) * 16 + (rows, places)
    out_specs = (rows, places, rows) + (P(),) * 16
    count = mesh.shape["batch"] * mesh.shape["seq"]
    return jax.shard_map(
        partial(body, count), mesh=mesh, in_specs=in_specs, out_specs=out_specs, check_vma=False
    )
```

```python
from functools import partial

import jax
import jax.numpy as jnp
from jax import lax
from jax.experimental import pallas as pl
from jax.experimental.pallas import tpu as pltpu
from jax.sharding import PartitionSpec as P

HD = 64
EPS = 1e-06
MASKED = -1e30
bf16 = jnp.bfloat16
f32 = jnp.float32
AXES = ("batch", "seq")
PAIR = 2 * HD
VMEM = pl.BlockSpec(memory_space=pltpu.VMEM)
SMEM = pl.BlockSpec(memory_space=pltpu.SMEM)
HBM = pl.BlockSpec(memory_space=pl.ANY)


def dot(left, right, left_dim=1, right_dim=0):
    dims = (((left_dim,), (right_dim,)), ((), ()))
    return lax.dot_general(left, right, dims, preferred_element_type=f32)


def fetch(source, target, sem):
    copy = pltpu.make_async_copy(source, target, sem)
    copy.start()
    return copy


def column(row):
    return jnp.transpose(jnp.broadcast_to(row, (128, row.shape[1])))[:, :1]


def row_of(col):
    return jnp.transpose(jnp.broadcast_to(col, (col.shape[0], 128)))[:1]


def line(ref, part=slice(None)):
    return ref[part].reshape(1, -1)


def half_masks():
    lane = lax.broadcasted_iota(jnp.int32, (1, PAIR), 1)
    low = (lane < HD).astype(f32)
    return low.astype(bf16), (1.0 - low).astype(bf16)


def store_blocks(out, at, group, values, flip, rows):
    per = values.shape[0] // rows
    for i in range(per):
        place = (group * per + i) ^ flip
        start = pl.multiple_of(place * rows, 16)
        out[at, pl.ds(start, rows), :] = values[i * rows : (i + 1) * rows]


def project_kernel(x, wq, bq, wk, wv, bv, q, k, v):
    t = x[...]
    q[...] = (dot(t, wq[...]) + line(bq)).astype(bf16) * bf16(HD**-0.5)
    k[...] = dot(t, wk[...]).astype(bf16)
    v[...] = (dot(t, wv[...]) + line(bv)).astype(bf16)


def norm_forward(values):
    centered = values - jnp.mean(values, -1, keepdims=True)
    inverse = lax.rsqrt(jnp.mean(centered * centered, -1, keepdims=True) + EPS)
    return centered * inverse, inverse


def norm_backward(grad, gain, normed, inverse):
    g = grad * gain
    return inverse * (
        g - jnp.mean(g, -1, keepdims=True) - normed * jnp.mean(g * normed, -1, keepdims=True)
    )


def middle_kernel(
    scal, x_own, x_oth, q, k_own, v_own, seg, bv, b_out, gain1, shift1, b_up, b_down,
    gain2, shift2, w_head, cot, cot_weight, wk_h, wv_h, w_out_h, w_up_h, w_down_h,
    layer_out, term, probs_h, k_all, v_all, att_t, grad_sum1, grad_attn, grad_mix, vecs,
    send_d, keep_d, send_u, keep_u,
    wk, wv, w_out, w_up, w_down, v_t, probs, active, slope, packed_d, packed_u,
    w_sems, p_sems, o_sems,
):
    loads = [
        fetch(a, b, w_sems.at[n])
        for n, (a, b) in enumerate(
            ((wk_h, wk), (wv_h, wv), (w_out_h, w_out), (w_up_h, w_up), (w_down_h, w_down))
        )
    ]
    here, width = x_own.shape
    half, core = scal[0], scal[1]
    heads = width // HD
    loads[0].wait()
    loads[1].wait()
    other = x_oth[...]
    k_all[:here] = k_own[...]
    v_all[:here] = v_own[...]
    k_all[here:] = dot(other, wk[...]).astype(bf16)
    v_all[here:] = (dot(other, wv[...]) + line(bv)).astype(bf16)
    v_t[...] = jnp.transpose(v_all[...])

    own_ids = seg[:, pl.ds(pl.multiple_of(half * here, 128), here)].astype(f32)
    oth_ids = seg[:, pl.ds(pl.multiple_of((1 - half) * here, 128), here)].astype(f32)
    key_ids = jnp.concatenate([own_ids, oth_ids], 1)
    bias = jnp.where(column(key_ids) == own_ids, 0.0, MASKED)
    masks = half_masks()
    stores = []
    for p in range(heads // 2):
        lanes = slice(p * PAIR, (p + 1) * PAIR)
        q_pair, k_pair = q[:, lanes], k_all[:, lanes]
        for e in range(2):
            h = 2 * p + e
            scores = dot(k_pair, q_pair * masks[e], 1, 1) + bias
            weights = jnp.exp(scores - jnp.max(scores, 0, keepdims=True))
            weights = weights * (1.0 / jnp.sum(weights, 0, keepdims=True))
            low = weights.astype(bf16)
            probs[h] = low
            att_t[h * HD : (h + 1) * HD] = dot(v_t[h * HD : (h + 1) * HD], low).astype(bf16)
        stores.append(fetch(probs.at[pl.ds(2 * p, 2)], probs_h.at[pl.ds(2 * p, 2)], p_sems.at[p]))

    loads[2].wait()
    attn_out = dot(att_t[...], w_out[...], 0, 0) + line(b_out)
    n1, i1 = norm_forward(x_own[...].astype(f32) + attn_out)
    first = n1 * line(gain1) + line(shift1)
    f_low = first.astype(bf16)

    loads[3].wait()
    loads[4].wait()
    down = first + line(b_down)
    chunk = 1024
    for j in range(w_up.shape[1] // chunk):
        cols = slice(j * chunk, (j + 1) * chunk)
        u = dot(f_low, w_up[:, cols]) + line(b_up, cols)
        cdf = 0.5 + 0.5 * lax.erf(u * (2.0**-0.5))
        pdf = jnp.exp(-0.5 * u * u) * 0.3989422804014327
        slope[:, cols] = (cdf + u * pdf).astype(bf16)
        act = (u * cdf).astype(bf16)
        active[:, cols] = act
        down = down + dot(act, w_down[cols, :])

    n2, i2 = norm_forward(down)
    second = n2 * line(gain2) + line(shift2)
    layer_out[...] = second.astype(bf16)
    head = line(w_head).astype(f32)
    logits = jnp.sum(second * head, -1, keepdims=True)
    softplus = jnp.maximum(logits, 0.0) + jnp.log1p(jnp.exp(-jnp.abs(logits)))
    term[...] = row_of(softplus)
    grad_logits = column(cot_weight[...]) * lax.logistic(logits)
    vecs[0:1] = jnp.sum(grad_logits * second, 0, keepdims=True)
    grad_second = cot[...].astype(f32) + grad_logits * head
    vecs[1:2] = jnp.sum(grad_second * n2, 0, keepdims=True)
    vecs[2:3] = jnp.sum(grad_second, 0, keepdims=True)
    g_sum2 = norm_backward(grad_second, line(gain2), n2, i2)
    g_down = g_sum2.astype(bf16)
    vecs[3:4] = jnp.sum(g_down.astype(f32), 0, keepdims=True)
    vecs[11:] = jnp.zeros((5, width), f32)

    rows = packed_d.shape[1] // BLOCKS
    outs = []
    halves = (1 - core, core)
    for e, which in enumerate(halves):
        for j in range(2):
            start = pl.multiple_of((which * 2 + j) * width, 128)
            grad = dot(active[:, pl.ds(start, width)], g_down, 0, 0).astype(bf16)
            store_blocks(packed_d, e, j, grad, scal[3 - e], rows)
        outs.append(fetch(packed_d.at[e], (send_d, keep_d)[e], o_sems.at[e]))

    first_t = jnp.transpose(f_low)
    grad_first = g_sum2
    for e, which in enumerate(halves):
        for j in range(2):
            start = pl.multiple_of((which * 2 + j) * width, 128)
            part = pl.ds(start, width)
            g_active = dot(g_down, w_down[part, :], 1, 1)
            g_upper = (g_active * slope[:, part].astype(f32)).astype(bf16)
            vecs[pl.ds(4 + which * 2 + j, 1), :] = jnp.sum(g_upper.astype(f32), 0, keepdims=True)
            grad = dot(first_t, g_upper).astype(bf16)
            store_blocks(packed_u, e, j, grad, scal[5 - e], rows)
            grad_first = grad_first + dot(g_upper, w_up[:, part], 1, 1)
        outs.append(fetch(packed_u.at[e], (send_u, keep_u)[e], o_sems.at[2 + e]))

    vecs[8:9] = jnp.sum(grad_first * n1, 0, keepdims=True)
    vecs[9:10] = jnp.sum(grad_first, 0, keepdims=True)
    g_sum1 = norm_backward(grad_first, line(gain1), n1, i1)
    grad_sum1[...] = g_sum1
    g_attn = g_sum1.astype(bf16)
    grad_attn[...] = g_attn
    vecs[10:11] = jnp.sum(g_attn.astype(f32), 0, keepdims=True)
    grad_mix[...] = dot(g_attn, w_out[...], 1, 1).astype(bf16)
    for copy in stores + outs:
        copy.wait()


def attention_back_kernel(
    scal, x_own, x_oth, q, k_all, v_all, probs_h, att_t, grad_attn, grad_mix, vecs, after,
    grad_query, grad_key, grad_value, extra, send_h, keep_h,
    probs, k_t, x_t, query_t, vec_all, packed, p_sems, o_sems,
):
    here = x_own.shape[0]
    core, flip_keep, flip_send = scal[1], scal[6], scal[7]
    width = q.shape[1]
    heads = width // HD
    loads = [
        fetch(probs_h.at[pl.ds(2 * p, 2)], probs.at[pl.ds(2 * p, 2)], p_sems.at[p])
        for p in range(heads // 2)
    ]
    x_t[:, :here] = jnp.transpose(x_own[...])
    x_t[:, here:] = jnp.transpose(x_oth[...])
    k_t[...] = jnp.transpose(k_all[...])
    masks = half_masks()
    for p in range(heads // 2):
        lanes = slice(p * PAIR, (p + 1) * PAIR)
        mix_pair, q_pair, v_pair = grad_mix[:, lanes], q[:, lanes], v_all[:, lanes]
        mixes = [mix_pair * m for m in masks]
        queries = [q_pair * m for m in masks]
        loads[p].wait()
        grads = []
        for e in range(2):
            h = 2 * p + e
            weights = probs[h].astype(f32)
            product = weights * dot(v_pair, mixes[e], 1, 1)
            delta = jnp.sum(product, 0, keepdims=True)
            grad_scores = (product - weights * delta).astype(bf16)
            grads.append(grad_scores)
            query_t[h * HD : (h + 1) * HD] = (
                dot(k_t[h * HD : (h + 1) * HD], grad_scores) * (HD**-0.5)
            ).astype(bf16)
        both = jnp.concatenate([probs[2 * p], probs[2 * p + 1]], 1)
        grad_value[:, lanes] = dot(both, jnp.concatenate(mixes, 0)).astype(bf16)
        grad_key[:, lanes] = dot(
            jnp.concatenate(grads, 1), jnp.concatenate(queries, 0)
        ).astype(bf16)
    grad_query[...] = jnp.transpose(query_t[...])

    vec_all[...] = vecs[...]
    vec_all[11:12] = jnp.sum(grad_query[...].astype(f32), 0, keepdims=True)
    vec_all[12:13] = jnp.sum(grad_value[...].astype(f32), 0, keepdims=True)
    extra_low = vec_all[...].astype(bf16)
    extra[...] = extra_low

    total = packed.shape[1] - 16
    rows = total // BLOCKS
    packed[0, total:] = extra_low
    outs = []
    for e, which in enumerate((1 - core, core)):
        part = pl.ds(pl.multiple_of(which * (width // 2), 16), width // 2)
        for n in range(4):
            if n == 0:
                grad = dot(x_t[part, :here], query_t[...], 1, 1)
            elif n == 1:
                grad = dot(att_t[part, :], grad_attn[...])
            else:
                grad = dot(x_t[part, :], (grad_key, grad_value)[n - 2][...])
            store_blocks(packed, e, n, grad.astype(bf16), (flip_send, flip_keep)[e], rows)
        if e == 0:
            outs.append(fetch(packed.at[0], send_h, o_sems.at[0]))
        else:
            outs.append(fetch(packed.at[1, pl.ds(0, total)], keep_h, o_sems.at[1]))
    for copy in outs:
        copy.wait()


def tokens_kernel(grad_sum1, grad_query, grad_key, grad_value, wq, wk, wv, after, own, other):
    here = grad_sum1.shape[0]
    w_key, w_value = wk[...], wv[...]
    other[...] = (
        dot(grad_key[here:], w_key, 1, 1) + dot(grad_value[here:], w_value, 1, 1)
    ).astype(bf16)
    own[...] = (
        grad_sum1[...]
        + dot(grad_query[...], wq[...], 1, 1)
        + dot(grad_key[:here], w_key, 1, 1)
        + dot(grad_value[:here], w_value, 1, 1)
    )


def unpack_kernel(parts, held, scal, *refs):
    sources, refs = refs[: len(parts)], refs[len(parts) + held :]
    outs, (mark, scratch, sems) = refs[:6], refs[6:]
    mark[...] = jnp.zeros_like(mark)
    width = sources[0].shape[1]
    rows = sources[0].shape[0] // 4
    half = width // 2
    for slot, (source, (n, own, quarter)) in enumerate(zip(sources, parts)):
        which = scal[1] if own else 1 - scal[1]
        flip = scal[2 + 2 * n + (not own)]
        place = quarter ^ (flip // 4)
        for i in range(4):
            start = pl.multiple_of((i ^ (flip % 4)) * rows, 16)
            scratch[slot, i * rows : (i + 1) * rows, :] = source[pl.ds(start, rows), :].astype(f32)
        part, sem = scratch.at[slot], sems.at[slot]
        start = pl.multiple_of((which * 2 + place) * width, 128)
        if n == 0:
            fetch(part, outs[0].at[pl.ds(start, width), :], sem)
        elif n == 1:
            fetch(part, outs[1].at[:, pl.ds(start, width)], sem)
        else:
            target = pl.ds(pl.multiple_of(which * half, 16), half)
            for group in range(2):
                @pl.when(place == group)
                def _():
                    for i in range(2):
                        fetch(
                            scratch.at[slot, pl.ds(i * half, half)],
                            outs[2 + 2 * group + i].at[target, :],
                            sem,
                        )
    for slot in range(len(parts)):
        part = scratch.at[slot]
        pltpu.make_async_copy(part, part, sems.at[slot]).wait()


def call(kernel, in_specs, out_shapes, out_specs, scratch, vmem, moved=0, aliases=None):
    return pl.pallas_call(
        kernel,
        in_specs=in_specs,
        out_shape=out_shapes,
        out_specs=out_specs,
        scratch_shapes=scratch,
        input_output_aliases=aliases or {},
        compiler_params=pltpu.CompilerParams(vmem_limit_bytes=vmem * 2**20),
        cost_estimate=pl.CostEstimate(flops=0, bytes_accessed=moved, transcendentals=0),
    )


SEQ, CORE, NEAR, LINE, FAR = range(5)

STEPS = (
    ((SEQ, LINE), (NEAR, SEQ), (LINE, NEAR)),
    ((LINE, NEAR), (SEQ, LINE), (NEAR, SEQ)),
    ((NEAR, SEQ), (LINE, NEAR), (SEQ, LINE)),
)
BLOCKS = 8
UNPACK_VMEM = 18


def flip_of(index, pairs, core):
    bits = [(index >> pair[core]) & 1 for pair in pairs]
    return sum(b << (len(pairs) - 1 - n) for n, b in enumerate(bits))


def swap(values, pair, count):
    perm = [(i, i ^ (1 << pair[(i >> CORE) & 1])) for i in range(count)]
    return lax.ppermute(values, AXES, perm)


class Order:
    def __init__(self):
        self.passed = []

    def after(self, values, before):
        values, before = lax.optimization_barrier((values, before))
        self.passed += before
        return values


def halve(keep, got, extra, more_halves):
    size = keep.shape[0]
    if extra is not None:
        extra = extra + got[size:]
    if not more_halves:
        return keep + got[:size], None, extra
    half = size // 2
    send = keep[half:] + got[half:size]
    if extra is not None:
        send = jnp.concatenate([send, extra], 0)
    return keep[:half] + got[:half], send, extra


def sum_stream(order, keep, send, pairs, more, count, extra=None, before=None, late=None):
    steps = ((CORE, CORE),) + pairs
    for n, pair in enumerate(steps):
        got = swap(send, pair, count)
        if n == 2 and before is not None:
            keep, got = order.after((keep, got), [before])
        keep, send, extra = halve(keep, got, extra, n < len(steps) - 1)
    size = keep.shape[0]
    for pair in more:
        both = keep if extra is None else jnp.concatenate([keep, extra], 0)
        both = both + swap(both, pair, count)
        keep, extra = both[:size], None if extra is None else both[size:]
    for n, pair in enumerate(reversed(pairs[1:])):
        got = swap(keep, pair, count)
        if n == 0 and late is not None:
            keep, got = order.after((keep, got), [late])
        keep = jnp.concatenate([keep, got], 0)
    return keep, swap(keep, pairs[0], count), swap(keep, (CORE, CORE), count), extra


def body(
    count, tokens, segment_ids, w_query, b_query, w_key, w_value, b_value, w_out, b_out,
    gain_attn, shift_attn, w_up, b_up, w_down, b_down, gain_ffn, shift_ffn, w_head, cot_out,
    cot_weight,
):
    row_count, here, width = tokens.shape
    hidden = w_up.shape[1]
    heads = width // HD
    keys = segment_ids.shape[1]
    bits = count.bit_length() - 1
    share = hidden // 2

    seq = lax.axis_index("seq")
    index = lax.axis_index("batch") * 2 + seq
    core = (index >> CORE) & 1
    more = [(b, b) for b in range(FAR, bits)]
    scal = [seq, core]
    for pairs in STEPS:
        flips = [flip_of(index, pairs, c) for c in (0, 1)]
        scal.append(jnp.where(core == 0, flips[0], flips[1]))
        scal.append(jnp.where(core == 0, flips[1], flips[0]))
    scal = jnp.stack([jnp.asarray(v, jnp.int32) for v in scal])

    x_own = tokens.reshape(here, width)
    x_oth = lax.ppermute(x_own, "seq", [(0, 1), (1, 0)])
    sds = jax.ShapeDtypeStruct
    dma = pltpu.SemaphoreType.DMA

    q, k_own, v_own = call(
        project_kernel,
        [VMEM] * 6,
        [sds((here, width), bf16)] * 3,
        [VMEM] * 3,
        [],
        56,
    )(x_own, w_query, b_query, w_key, w_value, b_value)

    square, up, down = (
        pltpu.VMEM(x, bf16) for x in ((width, width), (width, hidden), (hidden, width))
    )
    (
        layer_out, term, probs, k_all, v_all, att_t, grad_sum1, grad_attn, grad_mix, vecs,
        send_d, keep_d, send_u, keep_u,
    ) = call(
        middle_kernel,
        [SMEM] + [VMEM] * 17 + [HBM] * 5,
        [
            sds((here, width), bf16),
            sds((1, here), f32),
            sds((heads, keys, here), bf16),
            sds((keys, width), bf16),
            sds((keys, width), bf16),
            sds((width, here), bf16),
            sds((here, width), f32),
            sds((here, width), bf16),
            sds((here, width), bf16),
            sds((16, width), f32),
        ]
        + [sds((share, width), bf16)] * 4,
        [VMEM, VMEM, HBM] + [VMEM] * 7 + [HBM] * 4,
        [
            square,
            square,
            square,
            up,
            down,
            pltpu.VMEM((width, keys), bf16),
            pltpu.VMEM((heads, keys, here), bf16),
            pltpu.VMEM((here, hidden), bf16),
            pltpu.VMEM((here, hidden), bf16),
            pltpu.VMEM((2, share, width), bf16),
            pltpu.VMEM((2, share, width), bf16),
            dma((5,)),
            dma((heads // 2,)),
            dma((4,)),
        ],
        58,
    )(
        scal, x_own, x_oth, q, k_own, v_own, segment_ids, b_value, b_out, gain_attn, shift_attn,
        b_up, b_down, gain_ffn, shift_ffn, w_head, cot_out.reshape(here, width), cot_weight,
        w_key, w_value, w_out, w_up, w_down,
    )

    def unpack(parts, sources, held, after):
        targets = [(hidden, width), (width, hidden)] + [(width, width)] * 4
        *outs, mark = call(
            partial(unpack_kernel, parts, len(held) + len(after)),
            [SMEM] + [VMEM] * len(sources) + [HBM] * (len(held) + len(after)),
            [sds(x, f32) for x in targets] + [sds((8, 128), f32)],
            [pl.BlockSpec(memory_space=pltpu.HBM)] * 6 + [VMEM],
            [pltpu.VMEM((len(parts), width, width), f32), dma((len(parts),))],
            UNPACK_VMEM,
            0,
            {1 + len(sources) + i: i for i in range(len(held))},
        )(scal, *sources, *held, *after)
        return outs, mark

    grad_query, grad_key, grad_value, extra, send_q, keep_q = call(
        attention_back_kernel,
        [SMEM] + [VMEM] * 5 + [HBM] + [VMEM] * 4 + [HBM],
        [
            sds((here, width), bf16),
            sds((keys, width), bf16),
            sds((keys, width), bf16),
            sds((16, width), bf16),
            sds((share + 16, width), bf16),
            sds((share, width), bf16),
        ],
        [VMEM] * 4 + [HBM] * 2,
        [
            pltpu.VMEM((heads, keys, here), bf16),
            pltpu.VMEM((width, keys), bf16),
            pltpu.VMEM((width, keys), bf16),
            pltpu.VMEM((width, here), bf16),
            pltpu.VMEM((16, width), f32),
            pltpu.VMEM((2, share + 16, width), bf16),
            dma((heads // 2,)),
            dma((2,)),
        ],
        56,
    )(
        scal, x_own, x_oth, q, k_all, v_all, probs, att_t, grad_attn, grad_mix, vecs,
        send_u,
    )
    own, other = call(
        tokens_kernel,
        [VMEM] * 7 + [HBM],
        [sds((here, width), f32), sds((here, width), bf16)],
        [VMEM] * 2,
        [],
        16,
    )(grad_sum1, grad_query, grad_key, grad_value, w_query, w_key, w_value, extra)
    received = lax.ppermute(other, "seq", [(0, 1), (1, 0)])

    grad_tokens = own + received.astype(f32)

    order = Order()
    sums = [
        sum_stream(order, keep_d, send_d, STEPS[0], more, count, None, None, grad_tokens),
        sum_stream(order, keep_u, send_u, STEPS[1], more, count, None, other),
        sum_stream(order, keep_q, send_q, STEPS[2], more, count, extra),
    ]
    vec = sums[2][3].astype(f32)
    small = [vec[n] for n in range(13)] + [vec[4:8].reshape(-1)]
    early = [x for n in range(3) for x in (sums[n][0], sums[n][2])]
    small, early = lax.optimization_barrier((small, early))
    parts = tuple((n, o, 0) for n in range(3) for o in (True, False))
    outs, mark = unpack(parts, early, [], [])
    gots = order.after([sums[n][1] for n in range(3)], [mark])
    others = [swap(got, (CORE, CORE), count) for got in gots]
    outs, mark = unpack(tuple((n, True, 1) for n in range(3)), gots, outs, [])
    outs, mark = unpack(
        tuple((n, False, 1) for n in range(3)), others, outs, order.passed + [mark]
    )
    grad_w_down, grad_w_up, grad_w_query, grad_w_out, grad_w_key, grad_w_value = outs
    return (
        layer_out.reshape(row_count, here, width),
        term.reshape(row_count, here),
        grad_tokens.reshape(row_count, here, width),
        grad_w_query,
        small[11],
        grad_w_key,
        grad_w_value,
        small[12],
        grad_w_out,
        small[10],
        small[8],
        small[9],
        grad_w_up,
        small[13],
        grad_w_down,
        small[3],
        small[1],
        small[2],
        small[0],
    )


def solution(mesh):
    rows, places = P("batch", "seq", None), P("batch", "seq")
    in_specs = (rows, P("batch", None)) + (P(),) * 16 + (rows, places)
    out_specs = (rows, places, rows) + (P(),) * 16
    count = mesh.shape["batch"] * mesh.shape["seq"]
    return jax.shard_map(
        partial(body, count), mesh=mesh, in_specs=in_specs, out_specs=out_specs, check_vma=False
    )
```
